512 devices in a mesh: dp: 32 (over y, x, z_hi), tensor: 16 (over z_lo, core).
Axes of the slice: x: 4, y: 4, z: 16 (z_hi: 2, z_lo: 8; z = z_hi * 8 + z_lo), core: 2. Of those that a mesh axis runs over, the one named last changes fastest.
Arguments:
- inputs: bfloat16 [384, 5120], P('dp', 'tensor'), may hold values from -6 to 6
- w_gate: bfloat16 [5120, 27648], P('tensor', 'dp'), may hold values from -0.078125 to 0.078125
- w_up: bfloat16 [5120, 27648], P('tensor', 'dp'), may hold values from -0.078125 to 0.078125
- w_down: bfloat16 [27648, 5120], P('dp', 'tensor'), may hold values from -0.0390625 to 0.0390625
- out_grad: bfloat16 [384, 5120], P('dp', 'tensor'), may hold values from -6 to 6
- confidence: int32 [384], P('dp'), may hold values from 16 to 256
Outputs:
- grad_x: bfloat16 [384, 5120], P('dp', 'tensor')
- grad_gate: bfloat16 [5120, 27648], P('tensor', 'dp')
- grad_up: bfloat16 [5120, 27648], P('tensor', 'dp')
- grad_down: bfloat16 [27648, 5120], P('dp', 'tensor')
The draws below stay inside these ranges and needn't reach their ends.
All inputs are finite; a program needn't handle non-finite values.
Results may differ from the reference program's by a relative error of at most 0.0057.
Values may be sent and summed in bfloat16 or wider, within the bound.
A program may use at most 64 MiB of HBM per device.

```python
import jax
import jax.numpy as jnp

D = 5120
FF = 27648
TOKENS = 384


def with_ends(drawn, rng, smallest, high):
    shape = drawn.shape
    spot = [jax.random.randint(jax.random.fold_in(rng, axis), (), 0, shape[axis]) for axis in range(len(shape))]
    drawn = drawn.at[tuple(spot)].set(smallest)
    longest = shape.index(max(shape))
    spot[longest] = (spot[longest] + 1) % shape[longest]
    return drawn.at[tuple(spot)].set(high)


def block_scale(stream_key, extent, shards, smallest, largest):
    factor_of = 1.0
    for axis_at, blocks in shards:
        steps = jax.random.uniform(jax.random.fold_in(jax.random.fold_in(stream_key, 6), axis_at), (blocks,), jnp.float32, smallest / len(shards), largest / len(shards))
        factor_of = factor_of * jnp.repeat(jnp.exp(steps), extent[axis_at] // blocks).reshape((-1,) + (1,) * (len(extent) - 1 - axis_at))
    return factor_of


def centred(stream_key, dims, scale, most, pieces=(), held_as=jnp.bfloat16):
    entries = jax.random.normal(stream_key, dims, jnp.float32) * scale
    if len(pieces) > 0:
        entries = block_scale(stream_key, dims, pieces, -0.22, 0.18) * entries
    return jnp.clip(entries, min=-most, max=most).astype(held_as)


def setup_inputs(seed: int = 0) -> dict:
    key_of = jax.random.split(jax.random.key(seed), 7)
    return {
        "inputs": centred(key_of[0], (TOKENS, D), 1.0, 6.0, ((0, 32), (1, 16))),
        "w_gate": centred(key_of[1], (D, FF), D ** -0.5, 0.078125, ((0, 16), (1, 32))),
        "w_up": centred(key_of[2], (D, FF), D ** -0.5, 0.078125, ((0, 16), (1, 32))),
        "w_down": centred(key_of[3], (FF, D), FF ** -0.5, 0.0390625, ((0, 32), (1, 16))),
        "out_grad": centred(key_of[4], (TOKENS, D), 1.0, 6.0, ((0, 32), (1, 16))),
        "confidence": with_ends(jax.random.randint(key_of[5], (TOKENS,), 16, 257), jax.random.fold_in(key_of[5], 1), 16, 256).astype(jnp.int32),
    }


def reference(inputs, w_gate, w_up, w_down, out_grad, confidence):
    factor = confidence.astype(jnp.float32) / 256.0
    scaled = (out_grad.astype(jnp.float32) * factor[:, None]).astype(jnp.bfloat16)
    gate_pre = jnp.dot(inputs, w_gate, preferred_element_type=jnp.float32)
    up_pre = jnp.dot(inputs, w_up, preferred_element_type=jnp.float32)
    back_grad = jnp.dot(scaled, w_down.T, preferred_element_type=jnp.float32)
    logistic = jax.nn.sigmoid(gate_pre)
    swish = gate_pre * logistic
    hidden = (swish * up_pre).astype(jnp.bfloat16)
    up_grad = (back_grad * swish).astype(jnp.bfloat16)
    gate_grad = (back_grad * up_pre * logistic * (1.0 + gate_pre * (1.0 - logistic))).astype(jnp.bfloat16)
    grad_down = jnp.dot(hidden.T, scaled, preferred_element_type=jnp.float32).astype(jnp.bfloat16)
    grad_gate = jnp.dot(inputs.T, gate_grad, preferred_element_type=jnp.float32).astype(jnp.bfloat16)
    grad_up = jnp.dot(inputs.T, up_grad, preferred_element_type=jnp.float32).astype(jnp.bfloat16)
    total = jnp.dot(gate_grad, w_gate.T, preferred_element_type=jnp.float32)
    total = total + jnp.dot(up_grad, w_up.T, preferred_element_type=jnp.float32)
    grad_x = total.astype(jnp.bfloat16)
    return grad_x, grad_gate, grad_up, grad_down
```

```python
import functools

import jax
import jax.numpy as jnp
import numpy as np
from jax import lax
from jax.experimental import pallas as pl
from jax.experimental.pallas import tpu as pltpu
from jax.sharding import PartitionSpec as P

BF16, F32 = jnp.bfloat16, jnp.float32
NY, NX, NH = 4, 4, 2
LINE = 8
LEFT, RIGHT = 3, 4
ROWS = 12
SLOT = 16
TOKENS = NY * NX * NH * ROWS
BLOCK = 16
BLOCKS = TOKENS // BLOCK
CHUNK = 128
MESH = pl.DeviceIdType.MESH


def contract(left, right, left_dim, right_dim):
    return lax.dot_general(
        left, right, (((left_dim,), (right_dim,)), ((), ())), preferred_element_type=F32
    )


def kernel(
    x_ref, s_ref, wg_ref, wu_ref, wd_ref, pick_ref, drop_ref,
    dx_ref, dg_ref, du_ref, dd_ref,
    xg, sg, xc, sc, wg_far, wu_far, wd_far, part, rin, rout, crs, res,
    gxc, gxp, rx, sy, ry, sz, rz,
    w_sem, g1_sem, g2_sem, g3_sem, c_sem,
    rs_send, rs_recv, cross_recv, ag_send, ag_recv, x1_sem, x2_sem, x3_sem,
):
    dp, tensor = lax.axis_index("dp"), lax.axis_index("tensor")
    y, x, h = dp // (NX * NH), (dp // NH) % NX, dp % NH
    z, core = tensor // 2, tensor % 2

    def at_dp(y_, x_, h_):
        return {"dp": (y_ * NX + x_) * NH + h_, "tensor": tensor}

    def at_line(z_, core_):
        return {"dp": dp, "tensor": z_ * 2 + core_}

    def remote(src, dst, send, recv, device):
        return pltpu.make_async_remote_copy(
            src_ref=src, dst_ref=dst, send_sem=send, recv_sem=recv,
            device_id=device, device_id_type=MESH,
        )

    across = at_dp(y, x, 1 - h)
    x_peers = [at_dp(y, (x + k) % NX, h) for k in range(1, NX)]
    y_peers = [at_dp((y + k) % NY, x, h) for k in range(1, NY)]
    sibling = at_line(z, 1 - core)

    xg[y, x, h] = x_ref[...]
    sg[y, x, h] = s_ref[...]

    barrier = pltpu.get_barrier_semaphore()

    def greet(device):
        pl.semaphore_signal(barrier, inc=1, device_id=device, device_id_type=MESH)

    for device in [across, sibling] + x_peers + y_peers:
        greet(device)

    @pl.when(z > 0)
    def _():
        greet(at_line(z - 1, 0))
        greet(at_line(z - 1, 1))

    @pl.when(z < LINE - 1)
    def _():
        greet(at_line(z + 1, 0))
        greet(at_line(z + 1, 1))

    fixed = 2 + (NX - 1) + (NY - 1)

    @pl.when((z == 0) | (z == LINE - 1))
    def _():
        pl.semaphore_wait(barrier, fixed + 2)

    @pl.when((z > 0) & (z < LINE - 1))
    def _():
        pl.semaphore_wait(barrier, fixed + 4)

    weights = [
        remote(src, dst, w_sem.at[0, i], w_sem.at[1, i], sibling)
        for i, (src, dst) in enumerate(
            [(wg_ref, wg_far), (wu_ref, wu_far), (wd_ref, wd_far)]
        )
    ]

    first = [
        remote(ref.at[y, x, h], ref.at[y, x, h], g1_sem.at[0, i], g1_sem.at[1, i], across)
        for i, ref in enumerate((xg, sg))
    ]
    for copy in first:
        copy.start()

    @pl.when(core == 1)
    def _():
        for copy in weights:
            copy.start()

    for copy in first:
        copy.wait_recv()
    second = []
    for k in range(1, NX):
        second.append(
            remote(xg.at[y, x], xg.at[y, x], g2_sem.at[0, 0, k - 1], g2_sem.at[1, 0, k - 1], x_peers[k - 1])
        )
        second.append(
            remote(sg.at[y, x], sg.at[y, x], g2_sem.at[0, 1, k - 1], g2_sem.at[1, 1, k - 1], y_peers[k - 1])
        )
    for copy in second:
        copy.start()
    for copy in second:
        copy.wait_recv()
    third = []
    for k in range(1, NX):
        third.append(
            remote(xg.at[y], xg.at[y], g3_sem.at[0, 0, k - 1], g3_sem.at[1, 0, k - 1], y_peers[k - 1])
        )
        third.append(
            remote(sg.at[:, x], sg.at[:, x], g3_sem.at[0, 1, k - 1], g3_sem.at[1, 1, k - 1], x_peers[k - 1])
        )
    for copy in third:
        copy.start()
    for copy in third:
        copy.wait_recv()

    half, half_slots = TOKENS // 2, NY * NX * NH * SLOT // 2
    for gathered, packed in ((xg, xc), (sg, sc)):
        for i in range(2):
            slots = gathered[pl.ds(i * NY // 2, NY // 2)].reshape(half_slots, -1)
            packed[0, pl.ds(i * half, half)] = contract(pick_ref[...], slots, 1, 0).astype(BF16)

    columns = [
        remote(packed.at[0], packed.at[1], c_sem.at[0, i], c_sem.at[1, i], sibling)
        for i, packed in enumerate((xc, sc))
    ]

    outer = jnp.where(z <= LEFT, z - 1, z + 1)
    inner = jnp.where(z <= LEFT, z + 1, z - 1)
    is_end = (z == 0) | (z == LINE - 1)
    is_mid = (z == LEFT) | (z == RIGHT)

    def rows_of(m):
        return pl.ds(pl.multiple_of(m * BLOCK, BLOCK), BLOCK)

    def mine(m):
        return (m % 2) == (z - LEFT)

    def onward(m):
        return remote(
            rout.at[:, rows_of(m)], rin.at[:, rows_of(m)], rs_send.at[m], rs_recv.at[m],
            at_line(inner, 0),
        )

    def cross(m):
        return remote(
            rout.at[:, rows_of(m)], crs.at[:, rows_of(m)], rs_send.at[m], cross_recv.at[m],
            at_line(inner, 0),
        )

    def result(m, i, device):
        here = res.at[:, rows_of(m)]
        return remote(here, here, ag_send.at[i, m], ag_recv.at[m], device)

    def each_block(body):
        def step(m, carry):
            body(m)
            return carry

        lax.fori_loop(0, BLOCKS, step, 0)

    @pl.when(core == 1)
    def _():
        for copy in columns:
            copy.start()

        def forward(m):
            result(m, 0, sibling).wait_recv()

            @pl.when(jnp.logical_not(is_mid & mine(m)))
            def _():
                @pl.when(jnp.logical_not(is_end))
                def _():
                    result(m, 1, at_line(outer, 1)).start()

                result(m, 0, sibling).start()

        each_block(forward)

        def drain(m):
            @pl.when(jnp.logical_not(is_mid & mine(m)))
            def _():
                @pl.when(jnp.logical_not(is_end))
                def _():
                    result(m, 1, at_line(outer, 1)).wait_send()

                result(m, 0, sibling).wait_send()

        each_block(drain)
        for copy in columns:
            copy.wait_send()
        for copy in weights:
            copy.wait_send()

    @pl.when(core == 0)
    def _():
        for copy in weights:
            copy.wait_recv()
        for copy in columns:
            copy.wait_recv()

        def products(i, carry):
            rows = pl.ds(pl.multiple_of(i * CHUNK, CHUNK), CHUNK)
            part[0, rows] = contract(xc[0, rows], wg_ref[...], 1, 0) + contract(
                xc[1, rows], wg_far[...], 1, 0
            )
            part[1, rows] = contract(xc[0, rows], wu_ref[...], 1, 0) + contract(
                xc[1, rows], wu_far[...], 1, 0
            )
            part[2, rows] = contract(sc[0, rows], wd_ref[...], 1, 1) + contract(
                sc[1, rows], wd_far[...], 1, 1
            )

            @pl.when(is_end)
            def _():
                def send(k, inside):
                    m = i * (CHUNK // BLOCK) + k
                    rout[:, rows_of(m)] = part[:, rows_of(m)].astype(BF16)
                    onward(m).start()
                    return inside

                lax.fori_loop(0, CHUNK // BLOCK, send, 0)

            return carry

        lax.fori_loop(0, TOKENS // CHUNK, products, 0)

        @pl.when(jnp.logical_not(is_end | is_mid))
        def _():
            def add(m):
                onward(m).wait_recv()
                rout[:, rows_of(m)] = (
                    part[:, rows_of(m)] + rin[:, rows_of(m)].astype(F32)
                ).astype(BF16)
                onward(m).start()

            each_block(add)

        @pl.when(is_mid)
        def _():
            def finish(m):
                cross(m).wait_recv()
                rows = rows_of(m)
                gate_pre, up_pre, back_grad = (
                    part[i, rows] + crs[i, rows].astype(F32) for i in range(3)
                )
                logistic = jax.nn.sigmoid(gate_pre)
                swish = gate_pre * logistic
                res[0, rows] = (swish * up_pre).astype(BF16)
                res[1, rows] = (
                    back_grad * up_pre * logistic * (1.0 + gate_pre * (1.0 - logistic))
                ).astype(BF16)
                res[2, rows] = (back_grad * swish).astype(BF16)
                result(m, 0, at_line(outer, 1)).start()
                result(m, 1, at_line(inner, 1)).start()
                result(m, 2, sibling).start()

            lag = 2

            def step(m, carry):
                @pl.when(m < BLOCKS)
                def _():
                    onward(m).wait_recv()
                    total = part[:, rows_of(m)] + rin[:, rows_of(m)].astype(F32)

                    @pl.when(mine(m))
                    def _():
                        part[:, rows_of(m)] = total

                    @pl.when(jnp.logical_not(mine(m)))
                    def _():
                        rout[:, rows_of(m)] = total.astype(BF16)
                        cross(m).start()

                @pl.when((m >= lag) & mine(m))
                def _():
                    finish(m - lag)

                return carry

            lax.fori_loop(0, BLOCKS + lag, step, 0)

        def take(m):
            @pl.when(jnp.logical_not(is_mid & mine(m)))
            def _():
                result(m, 0, sibling).wait_recv()

        each_block(take)

        def drain(m):
            @pl.when(is_mid & mine(m))
            def _():
                result(m, 0, at_line(outer, 1)).wait_send()
                result(m, 1, at_line(inner, 1)).wait_send()
                result(m, 2, sibling).wait_send()

            @pl.when(jnp.logical_not(is_mid & mine(m)))
            def _():
                onward(m).wait_send()

        each_block(drain)

    def back(i, carry):
        rows = pl.ds(pl.multiple_of(i * CHUNK, CHUNK), CHUNK)
        gxc[rows] = (
            contract(res[1, rows], wg_ref[...], 1, 1) + contract(res[2, rows], wu_ref[...], 1, 1)
        ).astype(BF16)
        return carry

    lax.fori_loop(0, TOKENS // CHUNK, back, 0)
    for i in range(2):
        gxp[pl.ds(i * NY // 2, NY // 2)] = (
            contract(drop_ref[...], gxc[pl.ds(i * half, half)], 1, 0)
            .astype(BF16)
            .reshape(NY // 2, NX, NH, SLOT, -1)
        )
    along_x = [
        remote(gxp.at[:, (x + k) % NX], rx.at[k - 1], x1_sem.at[0, k - 1], x1_sem.at[1, k - 1], x_peers[k - 1])
        for k in range(1, NX)
    ]
    for copy in along_x:
        copy.start()
    dg_ref[...] = contract(xc[0], res[1], 0, 0).astype(BF16)
    for copy in along_x:
        copy.wait_recv()
    sy[...] = gxp[:, x].astype(F32) + rx[0].astype(F32) + rx[1].astype(F32) + rx[2].astype(F32)
    along_y = [
        remote(sy.at[(y + k) % NY], ry.at[k - 1], x2_sem.at[0, k - 1], x2_sem.at[1, k - 1], y_peers[k - 1])
        for k in range(1, NY)
    ]
    for copy in along_y:
        copy.start()
    du_ref[...] = contract(xc[0], res[2], 0, 0).astype(BF16)
    for copy in along_y:
        copy.wait_recv()
    sz[...] = sy[y] + ry[0] + ry[1] + ry[2]
    last = remote(sz.at[1 - h], rz, x3_sem.at[0], x3_sem.at[1], across)
    last.start()
    dd_ref[...] = contract(res[0], sc[0], 0, 0).astype(BF16)
    last.wait_recv()
    dx_ref[...] = (sz[h] + rz[...])[:ROWS].astype(BF16)

    for copy in first + second + third + along_x + along_y + [last]:
        copy.wait_send()


def local(inputs, w_gate, w_up, w_down, out_grad, confidence):
    depth, width = w_gate.shape
    factor = confidence.astype(F32) / 256.0
    scaled = (out_grad.astype(F32) * factor[:, None]).astype(BF16)
    padding = ((0, SLOT - ROWS), (0, 0))
    half = TOKENS // 2
    row = np.arange(half)
    pick = np.zeros((half, half // ROWS * SLOT), np.float32)
    pick[row, row // ROWS * SLOT + row % ROWS] = 1.0
    vmem = pl.BlockSpec(memory_space=pltpu.VMEM)
    slots = (NY, NX, NH, SLOT, depth)
    wide = (3, TOKENS, width)
    return pl.pallas_call(
        kernel,
        out_shape=(
            jax.ShapeDtypeStruct(inputs.shape, BF16),
            jax.ShapeDtypeStruct(w_gate.shape, BF16),
            jax.ShapeDtypeStruct(w_up.shape, BF16),
            jax.ShapeDtypeStruct(w_down.shape, BF16),
        ),
        in_specs=[vmem] * 7,
        out_specs=(vmem,) * 4,
        scratch_shapes=[
            pltpu.VMEM(slots, BF16),
            pltpu.VMEM(slots, BF16),
            pltpu.VMEM((2, TOKENS, depth), BF16),
            pltpu.VMEM((2, TOKENS, depth), BF16),
            pltpu.VMEM((depth, width), BF16),
            pltpu.VMEM((depth, width), BF16),
            pltpu.VMEM((width, depth), BF16),
            pltpu.VMEM(wide, F32),
            pltpu.VMEM(wide, BF16),
            pltpu.VMEM(wide, BF16),
            pltpu.VMEM(wide, BF16),
            pltpu.VMEM(wide, BF16),
            pltpu.VMEM((TOKENS, depth), BF16),
            pltpu.VMEM(slots, BF16),
            pltpu.VMEM((NX - 1, NY, NH, SLOT, depth), BF16),
            pltpu.VMEM((NY, NH, SLOT, depth), F32),
            pltpu.VMEM((NY - 1, NH, SLOT, depth), F32),
            pltpu.VMEM((NH, SLOT, depth), F32),
            pltpu.VMEM((SLOT, depth), F32),
            pltpu.SemaphoreType.DMA((2, 3)),
            pltpu.SemaphoreType.DMA((2, 2)),
            pltpu.SemaphoreType.DMA((2, 2, NX - 1)),
            pltpu.SemaphoreType.DMA((2, 2, NX - 1)),
            pltpu.SemaphoreType.DMA((2, 2)),
            pltpu.SemaphoreType.DMA((BLOCKS,)),
            pltpu.SemaphoreType.DMA((BLOCKS,)),
            pltpu.SemaphoreType.DMA((BLOCKS,)),
            pltpu.SemaphoreType.DMA((3, BLOCKS)),
            pltpu.SemaphoreType.DMA((BLOCKS,)),
            pltpu.SemaphoreType.DMA((2, NX - 1)),
            pltpu.SemaphoreType.DMA((2, NY - 1)),
            pltpu.SemaphoreType.DMA((2,)),
        ],
        compiler_params=pltpu.CompilerParams(
            collective_id=0, has_side_effects=True, vmem_limit_bytes=48 << 20
        ),
        cost_estimate=pl.CostEstimate(
            flops=2 * TOKENS * depth * width * 11,
            bytes_accessed=12 * depth * width,
            transcendentals=0,
        ),
    )(
        jnp.pad(inputs, padding),
        jnp.pad(scaled, padding),
        w_gate,
        w_up,
        w_down,
        jnp.asarray(pick, BF16),
        jnp.asarray(pick.T, BF16),
    )


def solution(mesh):
    placed = (
        P("dp", "tensor"),
        P("tensor", "dp"),
        P("tensor", "dp"),
        P("dp", "tensor"),
        P("dp", "tensor"),
        P("dp"),
    )
    return jax.shard_map(
        local,
        mesh=mesh,
        in_specs=placed,
        out_specs=(P("dp", "tensor"), P("tensor", "dp"), P("tensor", "dp"), P("dp", "tensor")),
        check_vma=False,
    )
```

```python
import jax
import jax.numpy as jnp
import numpy as np
from jax import lax
from jax.experimental import pallas as pl
from jax.experimental.pallas import tpu as pltpu
from jax.sharding import PartitionSpec as P

BF16, F32 = jnp.bfloat16, jnp.float32
NY, NX, NH = 4, 4, 2
LINE = 8
LEFT, RIGHT = 3, 4
ROWS = 12
SLOT = 16
TOKENS = NY * NX * NH * ROWS
HALF = TOKENS // 2
BLOCK = 16
PAIRS = HALF // BLOCK // 2
BLOCKS = TOKENS // BLOCK
LEAD = 3
AG_LEAD = 2
MESH = pl.DeviceIdType.MESH


def contract(left, right, left_dim, right_dim):
    return lax.dot_general(
        left, right, (((left_dim,), (right_dim,)), ((), ())), preferred_element_type=F32
    )


def loop(start, stop, body):
    def step(i, carry):
        body(i)
        return carry

    lax.fori_loop(start, stop, step, 0)


def kernel(
    x_ref, og_ref, conf_ref, wg_hbm, wu_hbm, wd_hbm, pick_ref, drop_ref,
    dx_ref, dg_ref, du_ref, dd_ref,
    xb, sb, xg, sg, xc, sc, w, part, rin, rout, crs, res,
    gxp, rx, sy, ry, sz, rz,
    l_sem, w_sem, own_sem, z_sem, g1_sem, g2_sem, g3_sem, c_sem,
    rs_send, rs_recv, cross_recv, ag_send, ag_recv, x1_sem, x2_sem, x3_sem,
):
    dp, tensor = lax.axis_index("dp"), lax.axis_index("tensor")
    y, x, h = dp // (NX * NH), (dp // NH) % NX, dp % NH
    z, core = tensor // 2, tensor % 2

    def at_dp(y_, x_, h_, core_):
        return {"dp": (y_ * NX + x_) * NH + h_, "tensor": z * 2 + core_}

    def at_line(z_, core_):
        return {"dp": dp, "tensor": z_ * 2 + core_}

    def remote(src, dst, send, recv, device):
        return pltpu.make_async_remote_copy(
            src_ref=src, dst_ref=dst, send_sem=send, recv_sem=recv,
            device_id=device, device_id_type=MESH,
        )

    across = at_dp(y, x, 1 - h, core)
    x_peers = [at_dp(y, (x + k) % NX, h, core) for k in range(1, NX)]
    y_peers = [at_dp((y + k) % NY, x, h, core) for k in range(1, NY)]
    x_others = [at_dp(y, (x + k) % NX, h, 1 - core) for k in range(1, NX)]
    y_others = [at_dp((y + k) % NY, x, h, 1 - core) for k in range(1, NY)]
    sibling = at_line(z, 1 - core)

    barrier = pltpu.get_barrier_semaphore()

    def greet(device):
        pl.semaphore_signal(barrier, inc=1, device_id=device, device_id_type=MESH)

    greeted = [across, sibling] + x_peers + y_peers + x_others + y_others
    for device in greeted:
        greet(device)

    @pl.when(z > 0)
    def _():
        greet(at_line(z - 1, 0))
        greet(at_line(z - 1, 1))

    @pl.when(z < LINE - 1)
    def _():
        greet(at_line(z + 1, 0))
        greet(at_line(z + 1, 1))

    loads = [
        pltpu.make_async_copy(ref, w.at[0, i], l_sem.at[i])
        for i, ref in enumerate((wg_hbm, wu_hbm, wd_hbm))
    ]
    for copy in loads:
        copy.start()

    factor = conf_ref[...].astype(F32) / 256.0
    xb[...] = jnp.zeros_like(xb)
    sb[...] = jnp.zeros_like(sb)
    xb[pl.ds(0, ROWS)] = x_ref[...]
    sb[pl.ds(0, ROWS)] = (og_ref[...].astype(F32) * factor).astype(BF16)

    @pl.when(core == 1)
    def _():
        xg[0, y, x, 1] = xb[...]
        sg[0, y, x, 1] = sb[...]

    @pl.when((z == 0) | (z == LINE - 1))
    def _():
        pl.semaphore_wait(barrier, len(greeted) + 2)

    @pl.when((z > 0) & (z < LINE - 1))
    def _():
        pl.semaphore_wait(barrier, len(greeted) + 4)

    outer = jnp.where(z <= LEFT, z - 1, z + 1)
    inner = jnp.where(z <= LEFT, z + 1, z - 1)
    is_end = (z == 0) | (z == LINE - 1)
    is_mid = (z == LEFT) | (z == RIGHT)
    left_side = jnp.where(z <= LEFT, 1, 0)

    own = [
        remote(src, dst.at[0, y, x, 0], own_sem.at[0, i], own_sem.at[1, i], sibling)
        for i, (src, dst) in enumerate(((xb, xg), (sb, sg)))
    ]
    weights = remote(w.at[0], w.at[1], w_sem.at[0], w_sem.at[1], sibling)
    exchange = [
        remote(ref.at[0, y, x], ref.at[1, y, x], z_sem.at[0, i], z_sem.at[1, i], across)
        for i, ref in enumerate((xg, sg))
    ]

    def gather_first(half):
        copies = []
        for k in range(NX - 1):
            here = xg.at[half, y, x]
            copies.append(
                remote(here, here, g1_sem.at[half, 0, 0, k], g1_sem.at[half, 1, 0, k], x_peers[k])
            )
            here = sg.at[half, y, x]
            copies.append(
                remote(here, here, g1_sem.at[half, 0, 1, k], g1_sem.at[half, 1, 1, k], y_peers[k])
            )
        return copies

    def gather_last(half):
        copies = []
        for k in range(NX):
            here = xg.at[half, y]
            copies.append(
                remote(
                    here, here, g2_sem.at[half, 0, k], g2_sem.at[half, 1, k],
                    ([sibling] + y_others)[k],
                )
            )
            here = sg.at[half, :, x]
            copies.append(
                remote(
                    here, here, g3_sem.at[half, 0, k], g3_sem.at[half, 1, k],
                    ([sibling] + x_others)[k],
                )
            )
        return copies

    def half_rows(half):
        return pl.ds(half * HALF, HALF)

    def columns(half):
        return [
            remote(
                packed.at[1, half_rows(half)], packed.at[0, half_rows(half)],
                c_sem.at[half, 0, i], c_sem.at[half, 1, i], sibling,
            )
            for i, packed in enumerate((xc, sc))
        ]

    def rows_of(m):
        return pl.ds(pl.multiple_of(m * BLOCK, BLOCK), BLOCK)

    def mine(m):
        return (m % 2) == (z - LEFT)

    def onward(m):
        return remote(
            rout.at[:, rows_of(m)], rin.at[:, rows_of(m)], rs_send.at[m], rs_recv.at[m],
            at_line(inner, 0),
        )

    def cross(m):
        return remote(
            rout.at[:, rows_of(m)], crs.at[:, rows_of(m)], rs_send.at[m], cross_recv.at[m],
            at_line(inner, 0),
        )

    def result(m, i, device):
        here = res.at[:, rows_of(m)]
        return remote(here, here, ag_send.at[i, m], ag_recv.at[m], device)

    def along_x(half):
        return [
            remote(
                gxp.at[half, :, (x + k) % NX], rx.at[half, k - 1],
                x1_sem.at[half, 0, k - 1], x1_sem.at[half, 1, k - 1], x_peers[k - 1],
            )
            for k in range(1, NX)
        ]

    def along_y(half):
        return [
            remote(
                sy.at[half, (y + k) % NY], ry.at[half, k - 1],
                x2_sem.at[half, 0, k - 1], x2_sem.at[half, 1, k - 1], y_peers[k - 1],
            )
            for k in range(1, NY)
        ]

    def back(half):
        rows = half_rows(half)
        total = (
            contract(res[1, rows], w[0, 0], 1, 1) + contract(res[2, rows], w[0, 1], 1, 1)
        ).astype(BF16)
        gxp[half] = contract(drop_ref[...], total, 1, 0).astype(BF16).reshape(NY, NX, SLOT, -1)
        for copy in along_x(half):
            copy.start()

    def sum_x(half):
        for copy in along_x(half):
            copy.wait_recv()
        total = gxp[half, :, x].astype(F32)
        for k in range(NX - 1):
            total = total + rx[half, k].astype(F32)
        sy[half] = total
        for copy in along_y(half):
            copy.start()

    def sum_y(half):
        for copy in along_y(half):
            copy.wait_recv()
        total = sy[half, y]
        for k in range(NY - 1):
            total = total + ry[half, k]
        sz[half] = total

    @pl.when(core == 1)
    def _():
        for copy in own:
            copy.wait_recv()
        for copy in gather_first(0) + exchange:
            copy.start()
        for copy in loads:
            copy.wait()
        weights.start()
        for copy in gather_first(0):
            copy.wait_recv()
        for copy in gather_last(0):
            copy.start()
        for copy in exchange:
            copy.wait_recv()
        for copy in gather_first(1):
            copy.start()
        for copy in gather_first(1):
            copy.wait_recv()
        for copy in gather_last(1):
            copy.start()

        def forward(m):
            result(m, 0, sibling).wait_recv()

            @pl.when(jnp.logical_not(is_mid & mine(m)))
            def _():
                @pl.when(jnp.logical_not(is_end))
                def _():
                    result(m, 1, at_line(outer, 1)).start()

                result(m, 0, sibling).start()

        for half in range(2):

            def step(s):
                @pl.when(s < PAIRS)
                def _():
                    forward(2 * (half * PAIRS + s) + 1 - left_side)

                @pl.when(s >= AG_LEAD)
                def _():
                    forward(2 * (half * PAIRS + s - AG_LEAD) + left_side)

            loop(0, PAIRS + AG_LEAD, step)
            back(half)

        for half in range(2):
            for copy in columns(half):
                copy.wait_recv()

    @pl.when(core == 0)
    def _():
        for copy in own:
            copy.start()

        def finish(m):
            onward(m).wait_recv()
            cross(m).wait_recv()
            rows = rows_of(m)
            gate_pre, up_pre, back_grad = (
                part[i, rows] + rin[i, rows].astype(F32) + crs[i, rows].astype(F32)
                for i in range(3)
            )
            logistic = jax.nn.sigmoid(gate_pre)
            swish = gate_pre * logistic
            res[0, rows] = (swish * up_pre).astype(BF16)
            res[1, rows] = (
                back_grad * up_pre * logistic * (1.0 + gate_pre * (1.0 - logistic))
            ).astype(BF16)
            res[2, rows] = (back_grad * swish).astype(BF16)
            result(m, 0, at_line(outer, 1)).start()
            result(m, 1, at_line(inner, 1)).start()
            result(m, 2, sibling).start()

        def add(m):
            @pl.when(is_end)
            def _():
                rout[:, rows_of(m)] = part[:, rows_of(m)].astype(BF16)
                onward(m).start()

            @pl.when(jnp.logical_not(is_end))
            def _():
                onward(m).wait_recv()
                rout[:, rows_of(m)] = (
                    part[:, rows_of(m)] + rin[:, rows_of(m)].astype(F32)
                ).astype(BF16)

                @pl.when(is_mid)
                def _():
                    cross(m).start()

                @pl.when(jnp.logical_not(is_mid))
                def _():
                    onward(m).start()

        for half in range(2):
            for copy in gather_last(half):
                copy.wait_recv()
            rows = half_rows(half)
            for gathered, packed in ((xg, xc), (sg, sc)):
                for side in range(2):
                    slots = gathered[half, :, :, side].reshape(NY * NX * SLOT, -1)
                    packed[side, rows] = contract(pick_ref[...], slots, 1, 0).astype(BF16)
            for copy in columns(half):
                copy.start()
            if half == 0:
                for copy in loads:
                    copy.wait()
                weights.wait_recv()
            for i, packed in enumerate((xc, xc, sc)):
                part[i, rows] = contract(packed[0, rows], w[0, i], 1, 0) + contract(
                    packed[1, rows], w[1, i], 1, 0
                )

            def step(s):
                @pl.when(s < PAIRS)
                def _():
                    add(2 * (half * PAIRS + s) + left_side)

                @pl.when(s >= LEAD)
                def _():
                    m = 2 * (half * PAIRS + s - LEAD) + 1 - left_side

                    @pl.when(is_mid)
                    def _():
                        finish(m)

                    @pl.when(jnp.logical_not(is_mid))
                    def _():
                        add(m)

            loop(0, PAIRS + LEAD, step)

        for half in range(2):

            def take(i):
                m = half * 2 * PAIRS + i

                @pl.when(jnp.logical_not(is_mid & mine(m)))
                def _():
                    result(m, 0, sibling).wait_recv()

            loop(0, 2 * PAIRS, take)
            back(half)

    sum_x(0)
    dg_ref[...] = contract(xc[0], res[1], 0, 0).astype(BF16)
    sum_x(1)
    du_ref[...] = contract(xc[0], res[2], 0, 0).astype(BF16)
    sum_y(1)
    last = remote(sz.at[1], rz, x3_sem.at[0], x3_sem.at[1], across)
    last.start()
    sum_y(0)
    dd_ref[...] = contract(sc[0], res[0], 0, 0).astype(BF16)

    @pl.when(core == 1)
    def _():
        for copy in exchange + [weights]:
            copy.wait_send()
        for half in range(2):
            for copy in gather_first(half) + gather_last(half):
                copy.wait_send()

        def drain(m):
            @pl.when(jnp.logical_not(is_mid & mine(m)))
            def _():
                @pl.when(jnp.logical_not(is_end))
                def _():
                    result(m, 1, at_line(outer, 1)).wait_send()

                result(m, 0, sibling).wait_send()

        loop(0, BLOCKS, drain)

    @pl.when(core == 0)
    def _():
        for copy in own:
            copy.wait_send()
        for half in range(2):
            for copy in columns(half):
                copy.wait_send()

        def drain(m):
            @pl.when(is_mid & mine(m))
            def _():
                result(m, 0, at_line(outer, 1)).wait_send()
                result(m, 1, at_line(inner, 1)).wait_send()
                result(m, 2, sibling).wait_send()

            @pl.when(jnp.logical_not(is_mid & mine(m)))
            def _():
                onward(m).wait_send()

        loop(0, BLOCKS, drain)

    for half in range(2):
        for copy in along_x(half) + along_y(half):
            copy.wait_send()
    last.wait()
    dx_ref[...] = (sz[0] + rz[...])[:ROWS].astype(BF16)


def local(inputs, w_gate, w_up, w_down, out_grad, confidence):
    depth, width = w_gate.shape
    row = np.arange(HALF)
    pick = np.zeros((HALF, HALF // ROWS * SLOT), np.float32)
    pick[row, row // ROWS * SLOT + row % ROWS] = 1.0
    vmem = pl.BlockSpec(memory_space=pltpu.VMEM)
    hbm = pl.BlockSpec(memory_space=pl.ANY)
    slots = (2, NY, NX, 2, SLOT, depth)
    wide = (3, TOKENS, width)
    dma = pltpu.SemaphoreType.DMA
    grad_x, grad_gate, grad_up, grad_down = pl.pallas_call(
        kernel,
        out_shape=(
            jax.ShapeDtypeStruct(inputs.shape, BF16),
            jax.ShapeDtypeStruct(w_gate.shape, BF16),
            jax.ShapeDtypeStruct(w_up.shape, BF16),
            jax.ShapeDtypeStruct((depth, width), BF16),
        ),
        in_specs=[vmem] * 3 + [hbm] * 3 + [vmem] * 2,
        out_specs=(vmem,) * 4,
        scratch_shapes=[
            pltpu.VMEM((SLOT, depth), BF16),
            pltpu.VMEM((SLOT, depth), BF16),
            pltpu.VMEM(slots, BF16),
            pltpu.VMEM(slots, BF16),
            pltpu.VMEM((2, TOKENS, depth), BF16),
            pltpu.VMEM((2, TOKENS, depth), BF16),
            pltpu.VMEM((2, 3, depth, width), BF16),
            pltpu.VMEM(wide, F32),
            pltpu.VMEM(wide, BF16),
            pltpu.VMEM(wide, BF16),
            pltpu.VMEM(wide, BF16),
            pltpu.VMEM(wide, BF16),
            pltpu.VMEM((2, NY, NX, SLOT, depth), BF16),
            pltpu.VMEM((2, NX - 1, NY, SLOT, depth), BF16),
            pltpu.VMEM((2, NY, SLOT, depth), F32),
            pltpu.VMEM((2, NY - 1, SLOT, depth), F32),
            pltpu.VMEM((2, SLOT, depth), F32),
            pltpu.VMEM((SLOT, depth), F32),
            dma((3,)),
            dma((2,)),
            dma((2, 2)),
            dma((2, 2)),
            dma((2, 2, 2, NX - 1)),
            dma((2, 2, NX)),
            dma((2, 2, NX)),
            dma((2, 2, 2)),
            dma((BLOCKS,)),
            dma((BLOCKS,)),
            dma((BLOCKS,)),
            dma((3, BLOCKS)),
            dma((BLOCKS,)),
            dma((2, 2, NX - 1)),
            dma((2, 2, NY - 1)),
            dma((2,)),
        ],
        compiler_params=pltpu.CompilerParams(
            collective_id=0, has_side_effects=True, vmem_limit_bytes=52 << 20
        ),
        cost_estimate=pl.CostEstimate(
            flops=2 * TOKENS * depth * width * 11,
            bytes_accessed=12 * depth * width,
            transcendentals=0,
        ),
    )(
        inputs,
        out_grad,
        confidence[:, None],
        w_gate,
        w_up,
        w_down.T,
        jnp.asarray(pick, BF16),
        jnp.asarray(pick.T, BF16),
    )
    return grad_x, grad_gate, grad_up, grad_down.T


def solution(mesh):
    placed = (
        P("dp", "tensor"),
        P("tensor", "dp"),
        P("tensor", "dp"),
        P("dp", "tensor"),
        P("dp", "tensor"),
        P("dp"),
    )
    return jax.shard_map(
        local,
        mesh=mesh,
        in_specs=placed,
        out_specs=(P("dp", "tensor"), P("tensor", "dp"), P("tensor", "dp"), P("dp", "tensor")),
        check_vma=False,
    )
```

```python
import jax
import jax.numpy as jnp
import numpy as np
from jax import lax
from jax.experimental import pallas as pl
from jax.experimental.pallas import tpu as pltpu
from jax.sharding import PartitionSpec as P

BF16, F32 = jnp.bfloat16, jnp.float32
NY, NX, NH = 4, 4, 2
LINE = 8
LEFT, RIGHT = 3, 4
ROWS = 12
SLOT = 16
TOKENS = NY * NX * NH * ROWS
HALF = TOKENS // 2
BLOCK = 16
BLOCKS = TOKENS // BLOCK
PAIRS = BLOCKS // 2
CUTS = (0, PAIRS // 4, 3 * PAIRS // 4, PAIRS)
LEAD = 2
MATRICES = 3
MESH = pl.DeviceIdType.MESH


def contract(left, right, left_dim, right_dim):
    return lax.dot_general(
        left, right, (((left_dim,), (right_dim,)), ((), ())), preferred_element_type=F32
    )


def loop(start, stop, body):
    def step(i, carry):
        body(i)
        return carry

    lax.fori_loop(start, stop, step, 0)


def kernel(
    x_ref, og_ref, conf_ref, wg_hbm, wu_hbm, wd_hbm, pick_ref, drop_ref,
    dx_ref, dg_ref, du_ref, dd_ref,
    xb, sb, xg, sg, xc, sc, w, part, rin, rout, crs, res,
    gxp, rx, sy, ry, sz, rz,
    l_sem, w_sem, own_sem, z_sem, g1_sem, g2_sem, g3_sem, c_sem,
    rs_send, rs_recv, cross_recv, ag_send, ag_recv, x1_sem, x2_sem, x3_sem,
):
    dp, tensor = lax.axis_index("dp"), lax.axis_index("tensor")
    y, x, h = dp // (NX * NH), (dp // NH) % NX, dp % NH
    z, core = tensor // 2, tensor % 2

    def at_dp(y_, x_, h_, core_):
        return {"dp": (y_ * NX + x_) * NH + h_, "tensor": z * 2 + core_}

    def at_line(z_, core_):
        return {"dp": dp, "tensor": z_ * 2 + core_}

    def remote(src, dst, send, recv, device):
        return pltpu.make_async_remote_copy(
            src_ref=src, dst_ref=dst, send_sem=send, recv_sem=recv,
            device_id=device, device_id_type=MESH,
        )

    across = at_dp(y, x, 1 - h, core)
    x_peers = [at_dp(y, (x + k) % NX, h, core) for k in range(1, NX)]
    y_peers = [at_dp((y + k) % NY, x, h, core) for k in range(1, NY)]
    x_others = [at_dp(y, (x + k) % NX, h, 1 - core) for k in range(1, NX)]
    y_others = [at_dp((y + k) % NY, x, h, 1 - core) for k in range(1, NY)]
    sibling = at_line(z, 1 - core)

    barrier = pltpu.get_barrier_semaphore()

    def greet(device):
        pl.semaphore_signal(barrier, inc=1, device_id=device, device_id_type=MESH)

    greeted = [across, sibling] + x_peers + y_peers + x_others + y_others
    for device in greeted:
        greet(device)

    @pl.when(z > 0)
    def _():
        greet(at_line(z - 1, 0))
        greet(at_line(z - 1, 1))

    @pl.when(z < LINE - 1)
    def _():
        greet(at_line(z + 1, 0))
        greet(at_line(z + 1, 1))

    loads = [
        pltpu.make_async_copy(ref, w.at[0, i], l_sem.at[i])
        for i, ref in enumerate((wg_hbm, wu_hbm, wd_hbm))
    ]
    for copy in loads:
        copy.start()

    factor = conf_ref[...].astype(F32) / 256.0
    xb[...] = jnp.zeros_like(xb)
    sb[...] = jnp.zeros_like(sb)
    xb[pl.ds(0, ROWS)] = x_ref[...]
    sb[pl.ds(0, ROWS)] = (og_ref[...].astype(F32) * factor).astype(BF16)

    @pl.when(core == 1)
    def _():
        xg[0, y, x, 1] = xb[...]
        sg[0, y, x, 1] = sb[...]

    @pl.when((z == 0) | (z == LINE - 1))
    def _():
        pl.semaphore_wait(barrier, len(greeted) + 2)

    @pl.when((z > 0) & (z < LINE - 1))
    def _():
        pl.semaphore_wait(barrier, len(greeted) + 4)

    outer = jnp.where(z <= LEFT, z - 1, z + 1)
    inner = jnp.where(z <= LEFT, z + 1, z - 1)
    is_end = (z == 0) | (z == LINE - 1)
    is_mid = (z == LEFT) | (z == RIGHT)
    left_side = jnp.where(z <= LEFT, 1, 0)

    own = [
        remote(src, dst.at[0, y, x, 0], own_sem.at[0, i], own_sem.at[1, i], sibling)
        for i, (src, dst) in enumerate(((xb, xg), (sb, sg)))
    ]
    weights = remote(w.at[0], w.at[1], w_sem.at[0], w_sem.at[1], sibling)
    exchange = [
        remote(ref.at[0, y, x], ref.at[1, y, x], z_sem.at[0, i], z_sem.at[1, i], across)
        for i, ref in enumerate((xg, sg))
    ]

    def gather_first(half):
        copies = []
        for k in range(NX - 1):
            here = xg.at[half, y, x]
            copies.append(
                remote(here, here, g1_sem.at[half, 0, 0, k], g1_sem.at[half, 1, 0, k], x_peers[k])
            )
            here = sg.at[half, y, x]
            copies.append(
                remote(here, here, g1_sem.at[half, 0, 1, k], g1_sem.at[half, 1, 1, k], y_peers[k])
            )
        return copies

    def gather_last(half):
        copies = []
        for k in range(NX):
            here = xg.at[half, y]
            copies.append(
                remote(
                    here, here, g2_sem.at[half, 0, k], g2_sem.at[half, 1, k],
                    ([sibling] + y_others)[k],
                )
            )
            here = sg.at[half, :, x]
            copies.append(
                remote(
                    here, here, g3_sem.at[half, 0, k], g3_sem.at[half, 1, k],
                    ([sibling] + x_others)[k],
                )
            )
        return copies

    columns = [
        remote(packed.at[1], packed.at[0], c_sem.at[0, i], c_sem.at[1, i], sibling)
        for i, packed in enumerate((xc, sc))
    ]

    def segment(i):
        start, stop = CUTS[i] * 2 * BLOCK, CUTS[i + 1] * 2 * BLOCK
        slots = (pl.ds(0, NY // 2), pl.ds(0, NY), pl.ds(NY // 2, NY // 2))[i]
        return pl.ds(start, stop - start), i % 2, slots, stop - start

    def rows_of(m):
        return pl.ds(pl.multiple_of(m * BLOCK, BLOCK), BLOCK)

    def mine(m):
        return (m % 2) == (z - LEFT)

    def onward(m, i):
        return remote(
            rout.at[i, rows_of(m)], rin.at[i, rows_of(m)], rs_send, rs_recv.at[m, i],
            at_line(inner, 0),
        )

    def cross(m, i):
        return remote(
            rout.at[i, rows_of(m)], crs.at[i, rows_of(m)], rs_send, cross_recv.at[m, i],
            at_line(inner, 0),
        )

    def result(m, i, way, device):
        here = res.at[i, rows_of(m)]
        return remote(here, here, ag_send.at[way], ag_recv.at[m, i], device)

    def sent(buffer, blocks, sem):
        rows = buffer.at[:, pl.ds(0, blocks * BLOCK)]
        remote(rows, rows, sem, sem, sibling).wait_send()

    def along_x(i):
        _, half, slots, _ = segment(i)
        return [
            remote(
                gxp.at[half, slots, (x + k) % NX], rx.at[half, k - 1, slots],
                x1_sem.at[i, 0, k - 1], x1_sem.at[i, 1, k - 1], x_peers[k - 1],
            )
            for k in range(1, NX)
        ]

    def along_y(half):
        return [
            remote(
                sy.at[half, (y + k) % NY], ry.at[half, k - 1],
                x2_sem.at[half, 0, k - 1], x2_sem.at[half, 1, k - 1], y_peers[k - 1],
            )
            for k in range(1, NY)
        ]

    def back(i):
        rows, half, slots, size = segment(i)
        total = (
            contract(res[1, rows], w[0, 0], 1, 1) + contract(res[2, rows], w[0, 1], 1, 1)
        ).astype(BF16)
        padded = size // ROWS * SLOT
        gxp[half, slots] = (
            contract(drop_ref[pl.ds(0, padded), pl.ds(0, size)], total, 1, 0)
            .astype(BF16)
            .reshape(-1, NX, SLOT, total.shape[-1])
        )
        for copy in along_x(i):
            copy.start()

    def sum_x(half):
        for i in (0, 2) if half == 0 else (1,):
            for copy in along_x(i):
                copy.wait_recv()
        total = gxp[half, :, x].astype(F32)
        for k in range(NX - 1):
            total = total + rx[half, k].astype(F32)
        sy[half] = total
        for copy in along_y(half):
            copy.start()

    def sum_y(half):
        for copy in along_y(half):
            copy.wait_recv()
        total = sy[half, y]
        for k in range(NY - 1):
            total = total + ry[half, k]
        sz[half] = total

    @pl.when(core == 1)
    def _():
        for copy in own:
            copy.wait_recv()
        for copy in gather_first(0) + exchange:
            copy.start()
        for copy in loads:
            copy.wait()
        weights.start()
        for copy in gather_first(0):
            copy.wait_recv()
        for copy in gather_last(0):
            copy.start()
        for copy in exchange:
            copy.wait_recv()
        for copy in gather_first(1):
            copy.start()
        for copy in gather_first(1):
            copy.wait_recv()
        for copy in gather_last(1):
            copy.start()

        def forward(m):
            for i in range(MATRICES):
                result(m, i, 0, sibling).wait_recv()

                @pl.when(jnp.logical_not(is_mid & mine(m)))
                def _():
                    result(m, i, 0, sibling).start()

                    @pl.when(jnp.logical_not(is_end))
                    def _():
                        result(m, i, 1, at_line(outer, 1)).start()

        def step(s):
            @pl.when(s < PAIRS)
            def _():
                forward(2 * s + 1 - left_side)

            @pl.when(s >= LEAD)
            def _():
                forward(2 * (s - LEAD) + left_side)

        loop(0, CUTS[1] + LEAD, step)
        back(0)
        loop(CUTS[1] + LEAD, CUTS[2] + LEAD, step)
        back(1)
        loop(CUTS[2] + LEAD, PAIRS, step)
        sum_x(1)
        loop(PAIRS, PAIRS + LEAD, step)
        back(2)
        for copy in columns:
            copy.wait_recv()

    @pl.when(core == 0)
    def _():
        for copy in own:
            copy.start()

        def finish(m):
            rows = rows_of(m)
            totals = []
            for i in range(MATRICES):
                onward(m, i).wait_recv()
                cross(m, i).wait_recv()
                totals.append(
                    part[i, rows] + rin[i, rows].astype(F32) + crs[i, rows].astype(F32)
                )
            gate_pre, up_pre, back_grad = totals
            logistic = jax.nn.sigmoid(gate_pre)
            swish = gate_pre * logistic
            gate_grad = back_grad * up_pre * logistic * (1.0 + gate_pre * (1.0 - logistic))
            for i, value in enumerate((swish * up_pre, gate_grad, back_grad * swish)):
                res[i, rows] = value.astype(BF16)
                result(m, i, 0, at_line(outer, 1)).start()
                result(m, i, 1, at_line(inner, 1)).start()
                result(m, i, 2, sibling).start()

        def add(m):
            rows = rows_of(m)
            for i in range(MATRICES):

                @pl.when(is_end)
                def _():
                    rout[i, rows] = part[i, rows].astype(BF16)
                    onward(m, i).start()

                @pl.when(jnp.logical_not(is_end))
                def _():
                    onward(m, i).wait_recv()
                    rout[i, rows] = (part[i, rows] + rin[i, rows].astype(F32)).astype(BF16)

                    @pl.when(is_mid)
                    def _():
                        cross(m, i).start()

                    @pl.when(jnp.logical_not(is_mid))
                    def _():
                        onward(m, i).start()

        def products(i):
            rows, half, slots, size = segment(i)
            padded = size // ROWS * SLOT
            for gathered, packed in ((xg, xc), (sg, sc)):
                for side in range(2):
                    block = gathered[half, slots, :, side].reshape(padded, -1)
                    packed[side, rows] = contract(
                        pick_ref[pl.ds(0, size), pl.ds(0, padded)], block, 1, 0
                    ).astype(BF16)
            if i == 0:
                for copy in loads:
                    copy.wait()
                weights.wait_recv()
            for j, packed in enumerate((xc, xc, sc)):
                part[j, rows] = contract(packed[0, rows], w[0, j], 1, 0) + contract(
                    packed[1, rows], w[1, j], 1, 0
                )

        def stream(first, last):
            def step(s):
                @pl.when(s < last)
                def _():
                    add(2 * s + left_side)

                @pl.when(s >= first + LEAD)
                def _():
                    m = 2 * (s - LEAD) + 1 - left_side

                    @pl.when(is_mid)
                    def _():
                        finish(m)

                    @pl.when(jnp.logical_not(is_mid))
                    def _():
                        add(m)

            loop(first, last + LEAD, step)

        for copy in gather_last(0):
            copy.wait_recv()
        products(0)
        stream(CUTS[0], CUTS[1])
        products(2)
        for copy in gather_last(1):
            copy.wait_recv()
        products(1)
        stream(CUTS[1], CUTS[3])
        for copy in columns:
            copy.start()

        def take(m):
            @pl.when(jnp.logical_not(is_mid & mine(m)))
            def _():
                for i in range(MATRICES):
                    result(m, i, 0, sibling).wait_recv()

        for i in range(3):
            loop(2 * CUTS[i], 2 * CUTS[i + 1], take)
            back(i)
            if i == 1:
                sum_x(1)

    sum_y(1)
    last = remote(sz.at[1], rz, x3_sem.at[0], x3_sem.at[1], across)
    last.start()
    dg_ref[...] = contract(xc[0], res[1], 0, 0).astype(BF16)
    sum_x(0)
    du_ref[...] = contract(xc[0], res[2], 0, 0).astype(BF16)
    sum_y(0)
    dd_ref[...] = contract(sc[0], res[0], 0, 0).astype(BF16)

    @pl.when(core == 1)
    def _():
        for copy in exchange + [weights]:
            copy.wait_send()
        for half in range(2):
            for copy in gather_first(half) + gather_last(half):
                copy.wait_send()

        @pl.when(is_mid)
        def _():
            sent(res, BLOCKS // 2, ag_send.at[0])
            sent(res, BLOCKS // 2, ag_send.at[1])

        @pl.when(jnp.logical_not(is_mid))
        def _():
            sent(res, BLOCKS, ag_send.at[0])

            @pl.when(jnp.logical_not(is_end))
            def _():
                sent(res, BLOCKS, ag_send.at[1])

    @pl.when(core == 0)
    def _():
        for copy in own + columns:
            copy.wait_send()

        @pl.when(is_mid)
        def _():
            sent(rout, BLOCKS // 2, rs_send)
            for way in range(3):
                sent(res, BLOCKS // 2, ag_send.at[way])

        @pl.when(jnp.logical_not(is_mid))
        def _():
            sent(rout, BLOCKS, rs_send)

    for i in range(3):
        for copy in along_x(i):
            copy.wait_send()
    for half in range(2):
        for copy in along_y(half):
            copy.wait_send()
    last.wait()
    dx_ref[...] = (sz[0] + rz[...])[:ROWS].astype(BF16)


def local(inputs, w_gate, w_up, w_down, out_grad, confidence):
    depth, width = w_gate.shape
    row = np.arange(HALF)
    pick = np.zeros((HALF, HALF // ROWS * SLOT), np.float32)
    pick[row, row // ROWS * SLOT + row % ROWS] = 1.0
    vmem = pl.BlockSpec(memory_space=pltpu.VMEM)
    hbm = pl.BlockSpec(memory_space=pltpu.HBM)
    slots = (2, NY, NX, 2, SLOT, depth)
    wide = (3, TOKENS, width)
    dma = pltpu.SemaphoreType.DMA
    grad_x, grad_gate, grad_up, grad_down = pl.pallas_call(
        kernel,
        out_shape=(
            jax.ShapeDtypeStruct(inputs.shape, BF16),
            jax.ShapeDtypeStruct(w_gate.shape, BF16),
            jax.ShapeDtypeStruct(w_up.shape, BF16),
            jax.ShapeDtypeStruct((depth, width), BF16),
        ),
        in_specs=[vmem] * 3 + [hbm] * 3 + [vmem] * 2,
        out_specs=(vmem,) * 4,
        scratch_shapes=[
            pltpu.VMEM((SLOT, depth), BF16),
            pltpu.VMEM((SLOT, depth), BF16),
            pltpu.VMEM(slots, BF16),
            pltpu.VMEM(slots, BF16),
            pltpu.VMEM((2, TOKENS, depth), BF16),
            pltpu.VMEM((2, TOKENS, depth), BF16),
            pltpu.VMEM((2, 3, depth, width), BF16),
            pltpu.VMEM(wide, F32),
            pltpu.VMEM(wide, BF16),
            pltpu.VMEM(wide, BF16),
            pltpu.VMEM(wide, BF16),
            pltpu.VMEM(wide, BF16),
            pltpu.VMEM((2, NY, NX, SLOT, depth), BF16),
            pltpu.VMEM((2, NX - 1, NY, SLOT, depth), BF16),
            pltpu.VMEM((2, NY, SLOT, depth), F32),
            pltpu.VMEM((2, NY - 1, SLOT, depth), F32),
            pltpu.VMEM((2, SLOT, depth), F32),
            pltpu.VMEM((SLOT, depth), F32),
            dma((3,)),
            dma((2,)),
            dma((2, 2)),
            dma((2, 2)),
            dma((2, 2, 2, NX - 1)),
            dma((2, 2, NX)),
            dma((2, 2, NX)),
            dma((2, 2)),
            dma,
            dma((BLOCKS, MATRICES)),
            dma((BLOCKS, MATRICES)),
            dma((3,)),
            dma((BLOCKS, MATRICES)),
            dma((3, 2, NX - 1)),
            dma((2, 2, NY - 1)),
            dma((2,)),
        ],
        compiler_params=pltpu.CompilerParams(
            collective_id=0, has_side_effects=True, vmem_limit_bytes=52 << 20
        ),
        cost_estimate=pl.CostEstimate(
            flops=2 * TOKENS * depth * width * 11,
            bytes_accessed=12 * depth * width,
            transcendentals=0,
        ),
    )(
        inputs,
        out_grad,
        confidence[:, None],
        w_gate,
        w_up,
        w_down.T,
        jnp.asarray(pick, BF16),
        jnp.asarray(pick.T, BF16),
    )
    return grad_x, grad_gate, grad_up, grad_down.T


def solution(mesh):
    placed = (
        P("dp", "tensor"),
        P("tensor", "dp"),
        P("tensor", "dp"),
        P("dp", "tensor"),
        P("dp", "tensor"),
        P("dp"),
    )
    return jax.shard_map(
        local,
        mesh=mesh,
        in_specs=placed,
        out_specs=(P("dp", "tensor"), P("tensor", "dp"), P("tensor", "dp"), P("dp", "tensor")),
        check_vma=False,
    )
```

```python
import jax
import jax.numpy as jnp
from jax import lax
from jax.experimental import pallas as pl
from jax.experimental.pallas import tpu as pltpu
from jax.sharding import PartitionSpec as P

BF16, F32 = jnp.bfloat16, jnp.float32
NY, NX, NH = 4, 4, 2
LINE = 8
LEFT, RIGHT = 3, 4
ROWS = 12
SLOT = 16
TOKENS = NY * NX * NH * ROWS
HALF = TOKENS // 2
BLOCK = 16
BLOCKS = TOKENS // BLOCK
CUTS = (0, BLOCKS // 4, 3 * BLOCKS // 4, BLOCKS)
LAG = 4
MATRICES = 3
MESH = pl.DeviceIdType.MESH


def contract(left, right, left_dim, right_dim):
    return lax.dot_general(
        left, right, (((left_dim,), (right_dim,)), ((), ())), preferred_element_type=F32
    )


def loop(start, stop, body):
    def step(i, carry):
        body(i)
        return carry

    lax.fori_loop(start, stop, step, 0)


def kernel(
    x_ref, og_ref, conf_ref, wg_hbm, wu_hbm, wd_hbm,
    dx_ref, dg_ref, du_ref, dd_ref,
    pick_ref, drop_ref, xb, sb, xg, sg, xc, sc, w, part, rin, rout, crs, res,
    gxp, rx, sy, ry, sz, rz,
    l_sem, w_sem, own_sem, z_sem, g1_sem, g2_sem, g3_sem, c_sem,
    rs_send, rs_recv, cross_recv, ag_send, ag_recv, x1_sem, x2_sem, x3_sem,
):
    dp, tensor = lax.axis_index("dp"), lax.axis_index("tensor")
    y, x, h = dp // (NX * NH), (dp // NH) % NX, dp % NH
    z, core = tensor // 2, tensor % 2

    def at_dp(y_, x_, h_, core_):
        return {"dp": (y_ * NX + x_) * NH + h_, "tensor": z * 2 + core_}

    def at_line(z_, core_):
        return {"dp": dp, "tensor": z_ * 2 + core_}

    def remote(src, dst, send, recv, device):
        return pltpu.make_async_remote_copy(
            src_ref=src, dst_ref=dst, send_sem=send, recv_sem=recv,
            device_id=device, device_id_type=MESH,
        )

    across = at_dp(y, x, 1 - h, core)
    across_other = at_dp(y, x, 1 - h, 1 - core)
    x_peers = [at_dp(y, (x + k) % NX, h, core) for k in range(1, NX)]
    y_peers = [at_dp((y + k) % NY, x, h, core) for k in range(1, NY)]
    x_others = [at_dp(y, (x + k) % NX, h, 1 - core) for k in range(1, NX)]
    y_others = [at_dp((y + k) % NY, x, h, 1 - core) for k in range(1, NY)]
    sibling = at_line(z, 1 - core)

    barrier = pltpu.get_barrier_semaphore()

    def greet(device):
        pl.semaphore_signal(barrier, inc=1, device_id=device, device_id_type=MESH)

    greeted = [across, across_other, sibling] + x_peers + y_peers + x_others + y_others
    for device in greeted:
        greet(device)

    @pl.when(z > 0)
    def _():
        greet(at_line(z - 1, 0))
        greet(at_line(z - 1, 1))

    @pl.when(z < LINE - 1)
    def _():
        greet(at_line(z + 1, 0))
        greet(at_line(z + 1, 1))

    loads = [
        pltpu.make_async_copy(ref, w.at[0, i], l_sem.at[i])
        for i, ref in enumerate((wg_hbm, wu_hbm, wd_hbm))
    ]
    for copy in loads:
        copy.start()

    place = [lax.broadcasted_iota(jnp.int32, (ROWS, ROWS), i) for i in range(2)]
    spread = jnp.where(place[0] == place[1], conf_ref[...].astype(F32) / 256.0, 0.0)
    factor = jnp.sum(spread, axis=1, keepdims=True)
    xb[...] = jnp.zeros_like(xb)
    sb[...] = jnp.zeros_like(sb)
    xb[pl.ds(0, ROWS)] = x_ref[...]
    sb[pl.ds(0, ROWS)] = (og_ref[...].astype(F32) * factor).astype(BF16)

    for ref, dim in ((pick_ref, 0), (drop_ref, 1)):
        dense = lax.broadcasted_iota(jnp.int32, ref.shape, dim).astype(F32)
        padded = lax.broadcasted_iota(jnp.int32, ref.shape, 1 - dim).astype(F32)
        slot = jnp.floor((dense + 0.5) / ROWS)
        ref[...] = jnp.where(padded == dense + slot * (SLOT - ROWS), 1.0, 0.0).astype(BF16)

    @pl.when(core == 1)
    def _():
        xg[0, y, x, 1] = xb[...]
        sg[0, y, x, 1] = sb[...]

    @pl.when((z == 0) | (z == LINE - 1))
    def _():
        pl.semaphore_wait(barrier, len(greeted) + 2)

    @pl.when((z > 0) & (z < LINE - 1))
    def _():
        pl.semaphore_wait(barrier, len(greeted) + 4)

    outer = jnp.where(z <= LEFT, z - 1, z + 1)
    inner = jnp.where(z <= LEFT, z + 1, z - 1)
    is_end = (z == 0) | (z == LINE - 1)
    is_mid = (z == LEFT) | (z == RIGHT)

    own = [
        remote(src, dst.at[0, y, x, 0], own_sem.at[0, i], own_sem.at[1, i], sibling)
        for i, (src, dst) in enumerate(((xb, xg), (sb, sg)))
    ]
    weights = remote(w.at[0], w.at[1], w_sem.at[0], w_sem.at[1], sibling)

    def exchange(side, target):
        return [
            remote(
                src, dst.at[1, y, x, side], z_sem.at[0, i, side], z_sem.at[1, i, side], target
            )
            for i, (src, dst) in enumerate(((xb, xg), (sb, sg)))
        ]

    def gather_first(half):
        copies = []
        for k in range(NX - 1):
            here = xg.at[half, y, x]
            copies.append(
                remote(here, here, g1_sem.at[half, 0, 0, k], g1_sem.at[half, 1, 0, k], x_peers[k])
            )
            here = sg.at[half, y, x]
            copies.append(
                remote(here, here, g1_sem.at[half, 0, 1, k], g1_sem.at[half, 1, 1, k], y_peers[k])
            )
        return copies

    def gather_last(half):
        copies = []
        for k in range(NX):
            here = xg.at[half, y]
            copies.append(
                remote(
                    here, here, g2_sem.at[half, 0, k], g2_sem.at[half, 1, k],
                    ([sibling] + y_others)[k],
                )
            )
            here = sg.at[half, :, x]
            copies.append(
                remote(
                    here, here, g3_sem.at[half, 0, k], g3_sem.at[half, 1, k],
                    ([sibling] + x_others)[k],
                )
            )
        return copies

    columns = [
        remote(packed.at[1], packed.at[0], c_sem.at[0, i], c_sem.at[1, i], sibling)
        for i, packed in enumerate((xc, sc))
    ]

    def segment(i):
        start, stop = CUTS[i] * BLOCK, CUTS[i + 1] * BLOCK
        slots = (pl.ds(0, NY // 2), pl.ds(0, NY), pl.ds(NY // 2, NY // 2))[i]
        return pl.ds(start, stop - start), i % 2, slots, stop - start

    def rows_of(m):
        return pl.ds(pl.multiple_of(m * BLOCK, BLOCK), BLOCK)

    def onward(m, i):
        return remote(
            rout.at[i, rows_of(m)], rin.at[i, rows_of(m)], rs_send, rs_recv.at[m, i],
            at_line(inner, 0),
        )

    def cross(m, i):
        return remote(
            rout.at[i, rows_of(m)], crs.at[i, rows_of(m)], rs_send, cross_recv.at[m, i],
            at_line(inner, 0),
        )

    def result(m, i, way, device):
        here = res.at[i, rows_of(m)]
        return remote(here, here, ag_send.at[way], ag_recv.at[m, i], device)

    def sent(buffer, sem):
        remote(buffer, buffer, sem, sem, sibling).wait_send()

    def along_x(i):
        _, half, slots, _ = segment(i)
        return [
            remote(
                gxp.at[half, slots, (x + k) % NX], rx.at[half, k - 1, slots],
                x1_sem.at[i, 0, k - 1], x1_sem.at[i, 1, k - 1], x_peers[k - 1],
            )
            for k in range(1, NX)
        ]

    def along_y(half):
        return [
            remote(
                sy.at[half, (y + k) % NY], ry.at[half, k - 1],
                x2_sem.at[half, 0, k - 1], x2_sem.at[half, 1, k - 1], y_peers[k - 1],
            )
            for k in range(1, NY)
        ]

    def back(i):
        rows, half, slots, size = segment(i)
        total = (
            contract(res[1, rows], w[0, 0], 1, 1) + contract(res[2, rows], w[0, 1], 1, 1)
        ).astype(BF16)
        padded = size // ROWS * SLOT
        gxp[half, slots] = (
            contract(drop_ref[pl.ds(0, padded), pl.ds(0, size)], total, 1, 0)
            .astype(BF16)
            .reshape(-1, NX, SLOT, total.shape[-1])
        )
        for copy in along_x(i):
            copy.start()

    def sum_x(half):
        for i in (0, 2) if half == 0 else (1,):
            for copy in along_x(i):
                copy.wait_recv()
        total = gxp[half, :, x].astype(F32)
        for k in range(NX - 1):
            total = total + rx[half, k].astype(F32)
        sy[half] = total
        for copy in along_y(half):
            copy.start()

    def sum_y(half):
        for copy in along_y(half):
            copy.wait_recv()
        total = sy[half, y]
        for k in range(NY - 1):
            total = total + ry[half, k]
        sz[half] = total

    @pl.when(core == 1)
    def _():
        for copy in exchange(1, across):
            copy.start()
        for copy in own:
            copy.wait_recv()
        for copy in gather_first(0):
            copy.start()
        for copy in loads:
            copy.wait()
        weights.start()
        for copy in gather_first(0):
            copy.wait_recv()
        for copy in gather_last(0):
            copy.start()
        for side in range(2):
            for copy in exchange(side, across):
                copy.wait_recv()
        for copy in gather_first(1):
            copy.start()
        for copy in gather_first(1):
            copy.wait_recv()
        for copy in gather_last(1):
            copy.start()

        def forward(m):
            for i in range(MATRICES):
                result(m, i, 0, sibling).wait_recv()

                @pl.when(jnp.logical_not(is_mid))
                def _():
                    result(m, i, 0, sibling).start()

                    @pl.when(jnp.logical_not(is_end))
                    def _():
                        result(m, i, 1, at_line(outer, 1)).start()

        loop(CUTS[0], CUTS[1], forward)
        back(0)
        loop(CUTS[1], CUTS[2], forward)
        back(1)
        loop(CUTS[2], CUTS[3] - 2, forward)
        sum_x(1)
        loop(CUTS[3] - 2, CUTS[3], forward)
        back(2)
        for copy in columns:
            copy.wait_recv()

    @pl.when(core == 0)
    def _():
        for copy in own + exchange(0, across_other):
            copy.start()

        def finish(m):
            rows = rows_of(m)
            totals = []
            for i in range(MATRICES):
                cross(m, i).wait_recv()
                totals.append(
                    part[i, rows] + rin[i, rows].astype(F32) + crs[i, rows].astype(F32)
                )
            gate_pre, up_pre, back_grad = totals
            logistic = jax.nn.sigmoid(gate_pre)
            swish = gate_pre * logistic
            gate_grad = back_grad * up_pre * logistic * (1.0 + gate_pre * (1.0 - logistic))
            for i, value in enumerate((swish * up_pre, gate_grad, back_grad * swish)):
                res[i, rows] = value.astype(BF16)
                result(m, i, 0, at_line(outer, 1)).start()
                result(m, i, 1, sibling).start()

        def add(m):
            rows = rows_of(m)
            for i in range(MATRICES):

                @pl.when(is_end)
                def _():
                    rout[i, rows] = part[i, rows].astype(BF16)
                    onward(m, i).start()

                @pl.when(jnp.logical_not(is_end))
                def _():
                    onward(m, i).wait_recv()
                    rout[i, rows] = (part[i, rows] + rin[i, rows].astype(F32)).astype(BF16)

                    @pl.when(is_mid)
                    def _():
                        cross(m, i).start()

                    @pl.when(jnp.logical_not(is_mid))
                    def _():
                        onward(m, i).start()

        def products(i):
            rows, half, slots, size = segment(i)
            padded = size // ROWS * SLOT
            for gathered, packed in ((xg, xc), (sg, sc)):
                for side in range(2):
                    block = gathered[half, slots, :, side].reshape(padded, -1)
                    packed[side, rows] = contract(
                        pick_ref[pl.ds(0, size), pl.ds(0, padded)], block, 1, 0
                    ).astype(BF16)
            if i == 0:
                for copy in loads:
                    copy.wait()
                weights.wait_recv()
            for j, packed in enumerate((xc, xc, sc)):
                part[j, rows] = contract(packed[0, rows], w[0, j], 1, 0) + contract(
                    packed[1, rows], w[1, j], 1, 0
                )

        def stream(first, last):
            @pl.when(jnp.logical_not(is_mid))
            def _():
                loop(first, last, add)

            @pl.when(is_mid)
            def _():
                def step(m):
                    @pl.when(m < last)
                    def _():
                        add(m)

                    @pl.when(m >= first + LAG)
                    def _():
                        finish(m - LAG)

                loop(first, last + LAG, step)

        for copy in gather_last(0):
            copy.wait_recv()
        products(0)
        stream(CUTS[0], CUTS[1])
        products(2)
        for copy in gather_last(1):
            copy.wait_recv()
        products(1)
        stream(CUTS[1], CUTS[3])
        for copy in columns:
            copy.start()

        def take(m):
            for i in range(MATRICES):
                result(m, i, 0, sibling).wait_recv()

        for i in range(3):

            @pl.when(jnp.logical_not(is_mid))
            def _():
                loop(CUTS[i], CUTS[i + 1], take)

            back(i)
            if i == 1:
                sum_x(1)

    sum_y(1)
    last = remote(sz.at[1], rz, x3_sem.at[0], x3_sem.at[1], across)
    last.start()
    dg_ref[...] = contract(xc[0], res[1], 0, 0).astype(BF16)
    sum_x(0)
    du_ref[...] = contract(xc[0], res[2], 0, 0).astype(BF16)
    sum_y(0)
    dd_ref[...] = contract(sc[0], res[0], 0, 0).astype(BF16)

    @pl.when(core == 1)
    def _():
        for copy in exchange(1, across) + [weights]:
            copy.wait_send()
        for half in range(2):
            for copy in gather_first(half) + gather_last(half):
                copy.wait_send()

        @pl.when(jnp.logical_not(is_mid))
        def _():
            sent(res, ag_send.at[0])

            @pl.when(jnp.logical_not(is_end))
            def _():
                sent(res, ag_send.at[1])

    @pl.when(core == 0)
    def _():
        for copy in own + exchange(0, across_other) + columns:
            copy.wait_send()
        sent(rout, rs_send)

        @pl.when(is_mid)
        def _():
            for way in range(2):
                sent(res, ag_send.at[way])

    for i in range(3):
        for copy in along_x(i):
            copy.wait_send()
    for half in range(2):
        for copy in along_y(half):
            copy.wait_send()
    last.wait()
    dx_ref[...] = (sz[0] + rz[...])[:ROWS].astype(BF16)


def local(inputs, w_gate, w_up, w_down, out_grad, confidence):
    depth, width = w_gate.shape
    vmem = pl.BlockSpec(memory_space=pltpu.VMEM)
    hbm = pl.BlockSpec(memory_space=pltpu.HBM)
    slots = (2, NY, NX, 2, SLOT, depth)
    wide = (3, TOKENS, width)
    dma = pltpu.SemaphoreType.DMA
    grad_x, grad_gate, grad_up, grad_down = pl.pallas_call(
        kernel,
        out_shape=(
            jax.ShapeDtypeStruct(inputs.shape, BF16),
            jax.ShapeDtypeStruct(w_gate.shape, BF16),
            jax.ShapeDtypeStruct(w_up.shape, BF16),
            jax.ShapeDtypeStruct((depth, width), BF16),
        ),
        in_specs=[vmem] * 3 + [hbm] * 3,
        out_specs=(vmem,) * 4,
        scratch_shapes=[
            pltpu.VMEM((HALF, HALF // ROWS * SLOT), BF16),
            pltpu.VMEM((HALF // ROWS * SLOT, HALF), BF16),
            pltpu.VMEM((SLOT, depth), BF16),
            pltpu.VMEM((SLOT, depth), BF16),
            pltpu.VMEM(slots, BF16),
            pltpu.VMEM(slots, BF16),
            pltpu.VMEM((2, TOKENS, depth), BF16),
            pltpu.VMEM((2, TOKENS, depth), BF16),
            pltpu.VMEM((2, 3, depth, width), BF16),
            pltpu.VMEM(wide, F32),
            pltpu.VMEM(wide, BF16),
            pltpu.VMEM(wide, BF16),
            pltpu.VMEM(wide, BF16),
            pltpu.VMEM(wide, BF16),
            pltpu.VMEM((2, NY, NX, SLOT, depth), BF16),
            pltpu.VMEM((2, NX - 1, NY, SLOT, depth), BF16),
            pltpu.VMEM((2, NY, SLOT, depth), F32),
            pltpu.VMEM((2, NY - 1, SLOT, depth), F32),
            pltpu.VMEM((2, SLOT, depth), F32),
            pltpu.VMEM((SLOT, depth), F32),
            dma((3,)),
            dma((2,)),
            dma((2, 2)),
            dma((2, 2, 2)),
            dma((2, 2, 2, NX - 1)),
            dma((2, 2, NX)),
            dma((2, 2, NX)),
            dma((2, 2)),
            dma,
            dma((BLOCKS, MATRICES)),
            dma((BLOCKS, MATRICES)),
            dma((2,)),
            dma((BLOCKS, MATRICES)),
            dma((3, 2, NX - 1)),
            dma((2, 2, NY - 1)),
            dma((2,)),
        ],
        compiler_params=pltpu.CompilerParams(
            collective_id=0, has_side_effects=True, vmem_limit_bytes=52 << 20
        ),
        cost_estimate=pl.CostEstimate(
            flops=2 * TOKENS * depth * width * 11,
            bytes_accessed=12 * depth * width,
            transcendentals=0,
        ),
    )(
        inputs,
        out_grad,
        confidence[None, :],
        w_gate,
        w_up,
        w_down.T,
    )
    return grad_x, grad_gate, grad_up, grad_down.T


def solution(mesh):
    placed = (
        P("dp", "tensor"),
        P("tensor", "dp"),
        P("tensor", "dp"),
        P("dp", "tensor"),
        P("dp", "tensor"),
        P("dp"),
    )
    return jax.shard_map(
        local,
        mesh=mesh,
        in_specs=placed,
        out_specs=(P("dp", "tensor"), P("tensor", "dp"), P("tensor", "dp"), P("dp", "tensor")),
        check_vma=False,
    )
```

```python
import jax
import jax.numpy as jnp
from jax import lax
from jax.experimental import pallas as pl
from jax.experimental.pallas import tpu as pltpu
from jax.sharding import PartitionSpec as P

BF16, F32 = jnp.bfloat16, jnp.float32
NY, NX, NH = 4, 4, 2
LINE = 8
LEFT, RIGHT = 3, 4
ROWS = 12
SLOT = 16
TOKENS = NY * NX * NH * ROWS
HALF = TOKENS // 2
BLOCK = 16
BLOCKS = TOKENS // BLOCK
CUTS = (0, BLOCKS // 4, 3 * BLOCKS // 4, BLOCKS)
LAG = 4
MATRICES = 3
MESH = pl.DeviceIdType.MESH


def contract(left, right, left_dim, right_dim):
    return lax.dot_general(
        left, right, (((left_dim,), (right_dim,)), ((), ())), preferred_element_type=F32
    )


def loop(start, stop, body):
    def step(i, carry):
        body(i)
        return carry

    lax.fori_loop(start, stop, step, 0)


def kernel(
    x_ref, og_ref, conf_ref, wg_hbm, wu_hbm, wd_hbm,
    dx_ref, dg_ref, du_ref, dd_ref,
    pick_ref, drop_ref, xb, sb, xg, sg, xc, sc, w, part, rin, rout, crs, res,
    gxp, rx, sy, ry, sz, rz,
    l_sem, w_sem, own_sem, z_sem, g1_sem, g2_sem, g3_sem, c_sem,
    rs_send, rs_recv, cross_recv, ag_send, ag_recv, x1_sem, x2_sem, x3_sem,
):
    dp, tensor = lax.axis_index("dp"), lax.axis_index("tensor")
    y, x, h = dp // (NX * NH), (dp // NH) % NX, dp % NH
    z, core = tensor // 2, tensor % 2

    def at_dp(y_, x_, h_, core_):
        return {"dp": (y_ * NX + x_) * NH + h_, "tensor": z * 2 + core_}

    def at_line(z_, core_):
        return {"dp": dp, "tensor": z_ * 2 + core_}

    def remote(src, dst, send, recv, device):
        return pltpu.make_async_remote_copy(
            src_ref=src, dst_ref=dst, send_sem=send, recv_sem=recv,
            device_id=device, device_id_type=MESH,
        )

    across = at_dp(y, x, 1 - h, core)
    across_other = at_dp(y, x, 1 - h, 1 - core)
    x_peers = [at_dp(y, (x + k) % NX, h, core) for k in range(1, NX)]
    y_peers = [at_dp((y + k) % NY, x, h, core) for k in range(1, NY)]
    x_others = [at_dp(y, (x + k) % NX, h, 1 - core) for k in range(1, NX)]
    y_others = [at_dp((y + k) % NY, x, h, 1 - core) for k in range(1, NY)]
    sibling = at_line(z, 1 - core)

    barrier = pltpu.get_barrier_semaphore()

    def greet(device):
        pl.semaphore_signal(barrier, inc=1, device_id=device, device_id_type=MESH)

    greeted = [across, across_other, sibling] + x_peers + y_peers + x_others + y_others
    for device in greeted:
        greet(device)

    @pl.when(z > 0)
    def _():
        greet(at_line(z - 1, 0))
        greet(at_line(z - 1, 1))

    @pl.when(z < LINE - 1)
    def _():
        greet(at_line(z + 1, 0))
        greet(at_line(z + 1, 1))

    loads = [
        pltpu.make_async_copy(ref, w.at[0, i], l_sem.at[i])
        for i, ref in enumerate((wg_hbm, wu_hbm, wd_hbm))
    ]
    for copy in loads:
        copy.start()

    place = [lax.broadcasted_iota(jnp.int32, (ROWS, ROWS), i) for i in range(2)]
    spread = jnp.where(place[0] == place[1], conf_ref[...].astype(F32) / 256.0, 0.0)
    factor = jnp.sum(spread, axis=1, keepdims=True)
    xb[...] = jnp.zeros_like(xb)
    sb[...] = jnp.zeros_like(sb)
    xb[pl.ds(0, ROWS)] = x_ref[...]
    sb[pl.ds(0, ROWS)] = (og_ref[...].astype(F32) * factor).astype(BF16)

    for ref, dim in ((pick_ref, 0), (drop_ref, 1)):
        dense = lax.broadcasted_iota(jnp.int32, ref.shape, dim).astype(F32)
        padded = lax.broadcasted_iota(jnp.int32, ref.shape, 1 - dim).astype(F32)
        slot = jnp.floor((dense + 0.5) / ROWS)
        ref[...] = jnp.where(padded == dense + slot * (SLOT - ROWS), 1.0, 0.0).astype(BF16)

    @pl.when(core == 1)
    def _():
        xg[0, y, x, 1] = xb[...]
        sg[0, y, x, 1] = sb[...]

    @pl.when((z == 0) | (z == LINE - 1))
    def _():
        pl.semaphore_wait(barrier, len(greeted) + 2)

    @pl.when((z > 0) & (z < LINE - 1))
    def _():
        pl.semaphore_wait(barrier, len(greeted) + 4)

    outer = jnp.where(z <= LEFT, z - 1, z + 1)
    inner = jnp.where(z <= LEFT, z + 1, z - 1)
    is_end = (z == 0) | (z == LINE - 1)
    is_mid = (z == LEFT) | (z == RIGHT)

    own = [
        remote(src, dst.at[0, y, x, 0], own_sem.at[0, i], own_sem.at[1, i], sibling)
        for i, (src, dst) in enumerate(((xb, xg), (sb, sg)))
    ]
    weights = remote(w.at[0], w.at[1], w_sem.at[0], w_sem.at[1], sibling)

    def exchange(side, target):
        return [
            remote(
                src, dst.at[1, y, x, side], z_sem.at[0, i, side], z_sem.at[1, i, side], target
            )
            for i, (src, dst) in enumerate(((xb, xg), (sb, sg)))
        ]

    def gather_first(half):
        copies = []
        for k in range(NX - 1):
            here = xg.at[half, y, x]
            copies.append(
                remote(here, here, g1_sem.at[half, 0, 0, k], g1_sem.at[half, 1, 0, k], x_peers[k])
            )
            here = sg.at[half, y, x]
            copies.append(
                remote(here, here, g1_sem.at[half, 0, 1, k], g1_sem.at[half, 1, 1, k], y_peers[k])
            )
        return copies

    def gather_last(half):
        copies = []
        for k in range(NX):
            here = xg.at[half, y]
            copies.append(
                remote(
                    here, here, g2_sem.at[half, 0, k], g2_sem.at[half, 1, k],
                    ([sibling] + y_others)[k],
                )
            )
            here = sg.at[half, :, x]
            copies.append(
                remote(
                    here, here, g3_sem.at[half, 0, k], g3_sem.at[half, 1, k],
                    ([sibling] + x_others)[k],
                )
            )
        return copies

    columns = [
        remote(packed.at[1], packed.at[0], c_sem.at[0, i], c_sem.at[1, i], sibling)
        for i, packed in enumerate((xc, sc))
    ]

    def segment(i):
        start, stop = CUTS[i] * BLOCK, CUTS[i + 1] * BLOCK
        slots = (pl.ds(0, NY // 2), pl.ds(0, NY), pl.ds(NY // 2, NY // 2))[i]
        return pl.ds(start, stop - start), i % 2, slots, stop - start

    def rows_of(m):
        return pl.ds(pl.multiple_of(m * BLOCK, BLOCK), BLOCK)

    def onward(m, i):
        return remote(
            rout.at[i, rows_of(m)], rin.at[i, rows_of(m)], rs_send, rs_recv.at[m, i],
            at_line(inner, 0),
        )

    def cross(m, i):
        return remote(
            rout.at[i, rows_of(m)], crs.at[i, rows_of(m)], rs_send, cross_recv.at[m, i],
            at_line(inner, 0),
        )

    def result(m, i, way, device):
        here = res.at[i, rows_of(m)]
        return remote(here, here, ag_send.at[way], ag_recv.at[m, i], device)

    def sent(buffer, sem):
        remote(buffer, buffer, sem, sem, sibling).wait_send()

    def along_x(i):
        _, half, slots, _ = segment(i)
        return [
            remote(
                gxp.at[half, slots, (x + k) % NX], rx.at[half, k - 1, slots],
                x1_sem.at[i, 0, k - 1], x1_sem.at[i, 1, k - 1], x_peers[k - 1],
            )
            for k in range(1, NX)
        ]

    def along_y(half):
        return [
            remote(
                sy.at[half, (y + k) % NY], ry.at[half, k - 1],
                x2_sem.at[half, 0, k - 1], x2_sem.at[half, 1, k - 1], y_peers[k - 1],
            )
            for k in range(1, NY)
        ]

    def back(i):
        rows, half, slots, size = segment(i)
        total = (
            contract(res[1, rows], w[0, 0], 1, 1) + contract(res[2, rows], w[0, 1], 1, 1)
        ).astype(BF16)
        padded = size // ROWS * SLOT
        gxp[half, slots] = (
            contract(drop_ref[pl.ds(0, padded), pl.ds(0, size)], total, 1, 0)
            .astype(BF16)
            .reshape(-1, NX, SLOT, total.shape[-1])
        )
        for copy in along_x(i):
            copy.start()

    def sum_x(half):
        for i in (0, 2) if half == 0 else (1,):
            for copy in along_x(i):
                copy.wait_recv()
        total = gxp[half, :, x].astype(F32)
        for k in range(NX - 1):
            total = total + rx[half, k].astype(F32)
        sy[half] = total
        for copy in along_y(half):
            copy.start()

    def sum_y(half):
        for copy in along_y(half):
            copy.wait_recv()
        total = sy[half, y]
        for k in range(NY - 1):
            total = total + ry[half, k]
        sz[half] = total

    @pl.when(core == 1)
    def _():
        for copy in exchange(1, across):
            copy.start()
        for copy in own:
            copy.wait_recv()
        for copy in gather_first(0):
            copy.start()
        for copy in loads:
            copy.wait()
        weights.start()
        for copy in gather_first(0):
            copy.wait_recv()
        for copy in gather_last(0):
            copy.start()
        for side in range(2):
            for copy in exchange(side, across):
                copy.wait_recv()
        for copy in gather_first(1):
            copy.start()
        for copy in gather_first(1):
            copy.wait_recv()
        for copy in gather_last(1):
            copy.start()

        def forward(m):
            for i in range(MATRICES):
                result(m, i, 0, sibling).wait_recv()

                @pl.when(jnp.logical_not(is_mid))
                def _():
                    result(m, i, 0, sibling).start()

                    @pl.when(jnp.logical_not(is_end))
                    def _():
                        result(m, i, 1, at_line(outer, 1)).start()

        loop(CUTS[0], CUTS[1], forward)
        back(0)
        loop(CUTS[1], CUTS[2], forward)
        back(1)
        loop(CUTS[2], CUTS[3], forward)
        back(2)
        sum_x(1)
        for copy in columns:
            copy.wait_recv()

    @pl.when(core == 0)
    def _():
        for copy in own + exchange(0, across_other):
            copy.start()

        def finish(m):
            rows = rows_of(m)
            totals = []
            for i in range(MATRICES):
                cross(m, i).wait_recv()
                totals.append(
                    part[i, rows] + rin[i, rows].astype(F32) + crs[i, rows].astype(F32)
                )
            gate_pre, up_pre, back_grad = totals
            logistic = jax.nn.sigmoid(gate_pre)
            swish = gate_pre * logistic
            gate_grad = back_grad * up_pre * logistic * (1.0 + gate_pre * (1.0 - logistic))
            for i, value in enumerate((swish * up_pre, gate_grad, back_grad * swish)):
                res[i, rows] = value.astype(BF16)
                result(m, i, 0, at_line(outer, 1)).start()
                result(m, i, 1, sibling).start()

        def add(m):
            rows = rows_of(m)
            for i in range(MATRICES):

                @pl.when(is_end)
                def _():
                    rout[i, rows] = part[i, rows].astype(BF16)
                    onward(m, i).start()

                @pl.when(jnp.logical_not(is_end))
                def _():
                    onward(m, i).wait_recv()
                    rout[i, rows] = (part[i, rows] + rin[i, rows].astype(F32)).astype(BF16)

                    @pl.when(is_mid)
                    def _():
                        cross(m, i).start()

                    @pl.when(jnp.logical_not(is_mid))
                    def _():
                        onward(m, i).start()

        def products(i):
            rows, half, slots, size = segment(i)
            padded = size // ROWS * SLOT
            for gathered, packed in ((xg, xc), (sg, sc)):
                for side in range(2):
                    block = gathered[half, slots, :, side].reshape(padded, -1)
                    packed[side, rows] = contract(
                        pick_ref[pl.ds(0, size), pl.ds(0, padded)], block, 1, 0
                    ).astype(BF16)
            if i == 0:
                for copy in loads:
                    copy.wait()
                weights.wait_recv()
            for j, packed in enumerate((xc, xc, sc)):
                part[j, rows] = contract(packed[0, rows], w[0, j], 1, 0) + contract(
                    packed[1, rows], w[1, j], 1, 0
                )

        def stream(first, last):
            @pl.when(jnp.logical_not(is_mid))
            def _():
                loop(first, last, add)

            @pl.when(is_mid)
            def _():
                def step(m):
                    @pl.when(m < last)
                    def _():
                        add(m)

                    @pl.when(m >= first + LAG)
                    def _():
                        finish(m - LAG)

                loop(first, last + LAG, step)

        for copy in gather_last(0):
            copy.wait_recv()
        products(0)
        stream(CUTS[0], CUTS[1])
        products(2)
        for copy in gather_last(1):
            copy.wait_recv()
        products(1)
        stream(CUTS[1], CUTS[3])
        for copy in columns:
            copy.start()

        def take(m):
            for i in range(MATRICES):
                result(m, i, 0, sibling).wait_recv()

        for i in range(3):

            @pl.when(jnp.logical_not(is_mid))
            def _():
                loop(CUTS[i], CUTS[i + 1], take)

            back(i)
            if i == 1:
                sum_x(1)

    sum_y(1)
    last = remote(sz.at[1], rz, x3_sem.at[0], x3_sem.at[1], across)
    last.start()
    dg_ref[...] = contract(xc[0], res[1], 0, 0).astype(BF16)
    sum_x(0)
    du_ref[...] = contract(xc[0], res[2], 0, 0).astype(BF16)
    sum_y(0)
    dd_ref[...] = contract(sc[0], res[0], 0, 0).astype(BF16)

    @pl.when(core == 1)
    def _():
        for copy in exchange(1, across) + [weights]:
            copy.wait_send()
        for half in range(2):
            for copy in gather_first(half) + gather_last(half):
                copy.wait_send()

        @pl.when(jnp.logical_not(is_mid))
        def _():
            sent(res, ag_send.at[0])

            @pl.when(jnp.logical_not(is_end))
            def _():
                sent(res, ag_send.at[1])

    @pl.when(core == 0)
    def _():
        for copy in own + exchange(0, across_other) + columns:
            copy.wait_send()
        sent(rout, rs_send)

        @pl.when(is_mid)
        def _():
            for way in range(2):
                sent(res, ag_send.at[way])

    for i in range(3):
        for copy in along_x(i):
            copy.wait_send()
    for half in range(2):
        for copy in along_y(half):
            copy.wait_send()
    last.wait()
    dx_ref[...] = (sz[0] + rz[...])[:ROWS].astype(BF16)


def local(inputs, w_gate, w_up, w_down, out_grad, confidence):
    depth, width = w_gate.shape
    vmem = pl.BlockSpec(memory_space=pltpu.VMEM)
    hbm = pl.BlockSpec(memory_space=pltpu.HBM)
    slots = (2, NY, NX, 2, SLOT, depth)
    wide = (3, TOKENS, width)
    dma = pltpu.SemaphoreType.DMA
    grad_x, grad_gate, grad_up, grad_down = pl.pallas_call(
        kernel,
        out_shape=(
            jax.ShapeDtypeStruct(inputs.shape, BF16),
            jax.ShapeDtypeStruct(w_gate.shape, BF16),
            jax.ShapeDtypeStruct(w_up.shape, BF16),
            jax.ShapeDtypeStruct((depth, width), BF16),
        ),
        in_specs=[vmem] * 3 + [hbm] * 3,
        out_specs=(vmem,) * 4,
        scratch_shapes=[
            pltpu.VMEM((HALF, HALF // ROWS * SLOT), BF16),
            pltpu.VMEM((HALF // ROWS * SLOT, HALF), BF16),
            pltpu.VMEM((SLOT, depth), BF16),
            pltpu.VMEM((SLOT, depth), BF16),
            pltpu.VMEM(slots, BF16),
            pltpu.VMEM(slots, BF16),
            pltpu.VMEM((2, TOKENS, depth), BF16),
            pltpu.VMEM((2, TOKENS, depth), BF16),
            pltpu.VMEM((2, 3, depth, width), BF16),
            pltpu.VMEM(wide, F32),
            pltpu.VMEM(wide, BF16),
            pltpu.VMEM(wide, BF16),
            pltpu.VMEM(wide, BF16),
            pltpu.VMEM(wide, BF16),
            pltpu.VMEM((2, NY, NX, SLOT, depth), BF16),
            pltpu.VMEM((2, NX - 1, NY, SLOT, depth), BF16),
            pltpu.VMEM((2, NY, SLOT, depth), F32),
            pltpu.VMEM((2, NY - 1, SLOT, depth), F32),
            pltpu.VMEM((2, SLOT, depth), F32),
            pltpu.VMEM((SLOT, depth), F32),
            dma((3,)),
            dma((2,)),
            dma((2, 2)),
            dma((2, 2, 2)),
            dma((2, 2, 2, NX - 1)),
            dma((2, 2, NX)),
            dma((2, 2, NX)),
            dma((2, 2)),
            dma,
            dma((BLOCKS, MATRICES)),
            dma((BLOCKS, MATRICES)),
            dma((2,)),
            dma((BLOCKS, MATRICES)),
            dma((3, 2, NX - 1)),
            dma((2, 2, NY - 1)),
            dma((2,)),
        ],
        compiler_params=pltpu.CompilerParams(
            collective_id=0, has_side_effects=True, vmem_limit_bytes=52 << 20
        ),
        cost_estimate=pl.CostEstimate(
            flops=2 * TOKENS * depth * width * 11,
            bytes_accessed=12 * depth * width,
            transcendentals=0,
        ),
    )(
        inputs,
        out_grad,
        confidence[None, :],
        w_gate,
        w_up,
        w_down.T,
    )
    return grad_x, grad_gate, grad_up, grad_down.T


def solution(mesh):
    placed = (
        P("dp", "tensor"),
        P("tensor", "dp"),
        P("tensor", "dp"),
        P("dp", "tensor"),
        P("dp", "tensor"),
        P("dp"),
    )
    return jax.shard_map(
        local,
        mesh=mesh,
        in_specs=placed,
        out_specs=(P("dp", "tensor"), P("tensor", "dp"), P("tensor", "dp"), P("dp", "tensor")),
        check_vma=False,
    )
```

```python
import jax
import jax.numpy as jnp
from jax import lax
from jax.experimental import pallas as pl
from jax.experimental.pallas import tpu as pltpu
from jax.sharding import PartitionSpec as P

BF16, F32 = jnp.bfloat16, jnp.float32
NY, NX, NH = 4, 4, 2
LINE = 8
LEFT, RIGHT = 3, 4
ROWS = 12
SLOT = 16
TOKENS = NY * NX * NH * ROWS
HALF = TOKENS // 2
BLOCK = 16
BLOCKS = TOKENS // BLOCK
CUTS = (0, BLOCKS // 8, 5 * BLOCKS // 8, BLOCKS)
LAG = 4
MATRICES = 3
MESH = pl.DeviceIdType.MESH


def contract(left, right, left_dim, right_dim):
    return lax.dot_general(
        left, right, (((left_dim,), (right_dim,)), ((), ())), preferred_element_type=F32
    )


def loop(start, stop, body):
    def step(i, carry):
        body(i)
        return carry

    lax.fori_loop(start, stop, step, 0)


def kernel(
    x_ref, og_ref, conf_ref, wg_hbm, wu_hbm, wd_hbm,
    dx_ref, dg_ref, du_ref, dd_ref,
    pick_ref, drop_ref, xb, sb, xg, sg, xc, sc, w, part, rin, rout, crs, res,
    gxp, rx, sy, ry, sz, rz,
    l_sem, w_sem, own_sem, z_sem, g1_sem, g2_sem, g3_sem, c_sem,
    rs_send, rs_recv, cross_recv, ag_send, ag_recv, x1_sem, x2_sem, x3_sem,
):
    dp, tensor = lax.axis_index("dp"), lax.axis_index("tensor")
    y, x, h = dp // (NX * NH), (dp // NH) % NX, dp % NH
    z, core = tensor // 2, tensor % 2

    def at_dp(y_, x_, h_, core_):
        return {"dp": (y_ * NX + x_) * NH + h_, "tensor": z * 2 + core_}

    def at_line(z_, core_):
        return {"dp": dp, "tensor": z_ * 2 + core_}

    def remote(src, dst, send, recv, device):
        return pltpu.make_async_remote_copy(
            src_ref=src, dst_ref=dst, send_sem=send, recv_sem=recv,
            device_id=device, device_id_type=MESH,
        )

    across = at_dp(y, x, 1 - h, core)
    across_other = at_dp(y, x, 1 - h, 1 - core)
    x_peers = [at_dp(y, (x + k) % NX, h, core) for k in range(1, NX)]
    y_peers = [at_dp((y + k) % NY, x, h, core) for k in range(1, NY)]
    x_others = [at_dp(y, (x + k) % NX, h, 1 - core) for k in range(1, NX)]
    y_others = [at_dp((y + k) % NY, x, h, 1 - core) for k in range(1, NY)]
    sibling = at_line(z, 1 - core)

    barrier = pltpu.get_barrier_semaphore()

    def greet(device):
        pl.semaphore_signal(barrier, inc=1, device_id=device, device_id_type=MESH)

    greeted = [across, across_other, sibling] + x_peers + y_peers + x_others + y_others
    for device in greeted:
        greet(device)

    @pl.when(z > 0)
    def _():
        greet(at_line(z - 1, 0))
        greet(at_line(z - 1, 1))

    @pl.when(z < LINE - 1)
    def _():
        greet(at_line(z + 1, 0))
        greet(at_line(z + 1, 1))

    loads = [
        pltpu.make_async_copy(ref, w.at[0, i], l_sem.at[i])
        for i, ref in enumerate((wg_hbm, wu_hbm, wd_hbm))
    ]
    for copy in loads:
        copy.start()

    place = [lax.broadcasted_iota(jnp.int32, (ROWS, ROWS), i) for i in range(2)]
    spread = jnp.where(place[0] == place[1], conf_ref[...].astype(F32) / 256.0, 0.0)
    factor = jnp.sum(spread, axis=1, keepdims=True)
    xb[...] = jnp.zeros_like(xb)
    sb[...] = jnp.zeros_like(sb)
    xb[pl.ds(0, ROWS)] = x_ref[...]
    sb[pl.ds(0, ROWS)] = (og_ref[...].astype(F32) * factor).astype(BF16)

    for ref, dim in ((pick_ref, 0), (drop_ref, 1)):
        dense = lax.broadcasted_iota(jnp.int32, ref.shape, dim).astype(F32)
        padded = lax.broadcasted_iota(jnp.int32, ref.shape, 1 - dim).astype(F32)
        slot = jnp.floor((dense + 0.5) / ROWS)
        ref[...] = jnp.where(padded == dense + slot * (SLOT - ROWS), 1.0, 0.0).astype(BF16)

    @pl.when(core == 1)
    def _():
        xg[0, y, x, 1] = xb[...]
        sg[0, y, x, 1] = sb[...]

    @pl.when((z == 0) | (z == LINE - 1))
    def _():
        pl.semaphore_wait(barrier, len(greeted) + 2)

    @pl.when((z > 0) & (z < LINE - 1))
    def _():
        pl.semaphore_wait(barrier, len(greeted) + 4)

    outer = jnp.where(z <= LEFT, z - 1, z + 1)
    inner = jnp.where(z <= LEFT, z + 1, z - 1)
    is_end = (z == 0) | (z == LINE - 1)
    is_mid = (z == LEFT) | (z == RIGHT)

    own = [
        remote(src, dst.at[0, y, x, 0], own_sem.at[0, i], own_sem.at[1, i], sibling)
        for i, (src, dst) in enumerate(((xb, xg), (sb, sg)))
    ]
    weights = remote(w.at[0], w.at[1], w_sem.at[0], w_sem.at[1], sibling)

    def exchange(side, target):
        return [
            remote(
                src, dst.at[1, y, x, side], z_sem.at[0, i, side], z_sem.at[1, i, side], target
            )
            for i, (src, dst) in enumerate(((xb, xg), (sb, sg)))
        ]

    def gather_first(half):
        copies = []
        for k in range(NX - 1):
            here = xg.at[half, y, x]
            copies.append(
                remote(here, here, g1_sem.at[half, 0, 0, k], g1_sem.at[half, 1, 0, k], x_peers[k])
            )
            here = sg.at[half, y, x]
            copies.append(
                remote(here, here, g1_sem.at[half, 0, 1, k], g1_sem.at[half, 1, 1, k], y_peers[k])
            )
        return copies

    def gather_last(half):
        copies = []
        for k in range(NX):
            here = xg.at[half, y]
            copies.append(
                remote(
                    here, here, g2_sem.at[half, 0, k], g2_sem.at[half, 1, k],
                    ([sibling] + y_others)[k],
                )
            )
            here = sg.at[half, :, x]
            copies.append(
                remote(
                    here, here, g3_sem.at[half, 0, k], g3_sem.at[half, 1, k],
                    ([sibling] + x_others)[k],
                )
            )
        return copies

    columns = [
        remote(packed.at[1], packed.at[0], c_sem.at[0, i], c_sem.at[1, i], sibling)
        for i, packed in enumerate((xc, sc))
    ]

    def segment(i):
        start, stop = CUTS[i] * BLOCK, CUTS[i + 1] * BLOCK
        slots = (pl.ds(0, 1), pl.ds(0, NY), pl.ds(1, NY - 1))[i]
        return pl.ds(start, stop - start), i % 2, slots, stop - start

    def rows_of(m):
        return pl.ds(pl.multiple_of(m * BLOCK, BLOCK), BLOCK)

    def onward(m, i):
        return remote(
            rout.at[i, rows_of(m)], rin.at[i, rows_of(m)], rs_send, rs_recv.at[m, i],
            at_line(inner, 0),
        )

    def cross(m, i):
        return remote(
            rout.at[i, rows_of(m)], crs.at[i, rows_of(m)], rs_send, cross_recv.at[m, i],
            at_line(inner, 0),
        )

    def result(m, i, way, device):
        here = res.at[i, rows_of(m)]
        return remote(here, here, ag_send.at[way], ag_recv.at[m, i], device)

    def sent(buffer, sem):
        remote(buffer, buffer, sem, sem, sibling).wait_send()

    def along_x(i):
        _, half, slots, _ = segment(i)
        return [
            remote(
                gxp.at[half, slots, (x + k) % NX], rx.at[half, k - 1, slots],
                x1_sem.at[i, 0, k - 1], x1_sem.at[i, 1, k - 1], x_peers[k - 1],
            )
            for k in range(1, NX)
        ]

    def along_y(half):
        return [
            remote(
                sy.at[half, (y + k) % NY], ry.at[half, k - 1],
                x2_sem.at[half, 0, k - 1], x2_sem.at[half, 1, k - 1], y_peers[k - 1],
            )
            for k in range(1, NY)
        ]

    def back(i):
        rows, half, slots, size = segment(i)
        total = (
            contract(res[1, rows], w[0, 0], 1, 1) + contract(res[2, rows], w[0, 1], 1, 1)
        ).astype(BF16)
        padded = size // ROWS * SLOT
        gxp[half, slots] = (
            contract(drop_ref[pl.ds(0, padded), pl.ds(0, size)], total, 1, 0)
            .astype(BF16)
            .reshape(-1, NX, SLOT, total.shape[-1])
        )
        for copy in along_x(i):
            copy.start()

    def sum_x(half):
        for i in (0, 2) if half == 0 else (1,):
            for copy in along_x(i):
                copy.wait_recv()
        total = gxp[half, :, x].astype(F32)
        for k in range(NX - 1):
            total = total + rx[half, k].astype(F32)
        sy[half] = total
        for copy in along_y(half):
            copy.start()

    def sum_y(half):
        for copy in along_y(half):
            copy.wait_recv()
        total = sy[half, y]
        for k in range(NY - 1):
            total = total + ry[half, k]
        sz[half] = total

    last = remote(sz.at[1], rz, x3_sem.at[0], x3_sem.at[1], across)

    @pl.when(core == 1)
    def _():
        for copy in exchange(1, across):
            copy.start()
        for copy in own:
            copy.wait_recv()
        for copy in gather_first(0):
            copy.start()
        for copy in loads:
            copy.wait()
        weights.start()
        for copy in gather_first(0):
            copy.wait_recv()
        for copy in gather_last(0):
            copy.start()
        for side in range(2):
            for copy in exchange(side, across):
                copy.wait_recv()
        for copy in gather_first(1):
            copy.start()
        for copy in gather_first(1):
            copy.wait_recv()
        for copy in gather_last(1):
            copy.start()

        def forward(m):
            for i in range(MATRICES):
                result(m, i, 0, sibling).wait_recv()

                @pl.when(jnp.logical_not(is_mid))
                def _():
                    result(m, i, 0, sibling).start()

                    @pl.when(jnp.logical_not(is_end))
                    def _():
                        result(m, i, 1, at_line(outer, 1)).start()

        loop(CUTS[0], CUTS[1], forward)
        back(0)
        loop(CUTS[1], CUTS[2], forward)
        back(1)
        loop(CUTS[2], CUTS[3] - 5, forward)
        sum_x(1)
        loop(CUTS[3] - 5, CUTS[3] - 1, forward)
        sum_y(1)
        last.start()
        loop(CUTS[3] - 1, CUTS[3], forward)
        back(2)
        for copy in columns:
            copy.wait_recv()

    @pl.when(core == 0)
    def _():
        for copy in own + exchange(0, across_other):
            copy.start()

        def finish(m):
            rows = rows_of(m)
            totals = []
            for i in range(MATRICES):
                cross(m, i).wait_recv()
                totals.append(
                    part[i, rows] + rin[i, rows].astype(F32) + crs[i, rows].astype(F32)
                )
            gate_pre, up_pre, back_grad = totals
            logistic = jax.nn.sigmoid(gate_pre)
            swish = gate_pre * logistic
            gate_grad = back_grad * up_pre * logistic * (1.0 + gate_pre * (1.0 - logistic))
            for i, value in enumerate((swish * up_pre, gate_grad, back_grad * swish)):
                res[i, rows] = value.astype(BF16)
                result(m, i, 0, at_line(outer, 1)).start()
                result(m, i, 1, sibling).start()

        def add(m):
            rows = rows_of(m)
            for i in range(MATRICES):

                @pl.when(is_end)
                def _():
                    rout[i, rows] = part[i, rows].astype(BF16)
                    onward(m, i).start()

                @pl.when(jnp.logical_not(is_end))
                def _():
                    onward(m, i).wait_recv()
                    rout[i, rows] = (part[i, rows] + rin[i, rows].astype(F32)).astype(BF16)

                    @pl.when(is_mid)
                    def _():
                        cross(m, i).start()

                    @pl.when(jnp.logical_not(is_mid))
                    def _():
                        onward(m, i).start()

        def products(i):
            rows, half, slots, size = segment(i)
            padded = size // ROWS * SLOT
            for gathered, packed in ((xg, xc), (sg, sc)):
                for side in range(2):
                    block = gathered[half, slots, :, side].reshape(padded, -1)
                    packed[side, rows] = contract(
                        pick_ref[pl.ds(0, size), pl.ds(0, padded)], block, 1, 0
                    ).astype(BF16)
            if i == 0:
                for copy in loads:
                    copy.wait()
                weights.wait_recv()
            for j, packed in enumerate((xc, xc, sc)):
                part[j, rows] = contract(packed[0, rows], w[0, j], 1, 0) + contract(
                    packed[1, rows], w[1, j], 1, 0
                )

        def stream(first, last):
            @pl.when(jnp.logical_not(is_mid))
            def _():
                loop(first, last, add)

            @pl.when(is_mid)
            def _():
                def step(m):
                    @pl.when(m < last)
                    def _():
                        add(m)

                    @pl.when(m >= first + LAG)
                    def _():
                        finish(m - LAG)

                loop(first, last + LAG, step)

        for copy in gather_last(0):
            copy.wait_recv()
        products(0)
        stream(CUTS[0], CUTS[1])
        products(2)
        for copy in gather_last(1):
            copy.wait_recv()
        products(1)
        stream(CUTS[1], CUTS[3])
        for copy in columns:
            copy.start()

        def take(m):
            for i in range(MATRICES):
                result(m, i, 0, sibling).wait_recv()

        for i in range(3):

            @pl.when(jnp.logical_not(is_mid))
            def _():
                loop(CUTS[i], CUTS[i + 1], take)

            if i == 2:
                sum_y(1)
                last.start()
            back(i)
            if i == 1:
                sum_x(1)

    dg_ref[...] = contract(xc[0], res[1], 0, 0).astype(BF16)
    sum_x(0)
    du_ref[...] = contract(xc[0], res[2], 0, 0).astype(BF16)
    sum_y(0)
    dd_ref[...] = contract(sc[0], res[0], 0, 0).astype(BF16)

    @pl.when(core == 1)
    def _():
        for copy in exchange(1, across) + [weights]:
            copy.wait_send()
        for half in range(2):
            for copy in gather_first(half) + gather_last(half):
                copy.wait_send()

        @pl.when(jnp.logical_not(is_mid))
        def _():
            sent(res, ag_send.at[0])

            @pl.when(jnp.logical_not(is_end))
            def _():
                sent(res, ag_send.at[1])

    @pl.when(core == 0)
    def _():
        for copy in own + exchange(0, across_other) + columns:
            copy.wait_send()
        sent(rout, rs_send)

        @pl.when(is_mid)
        def _():
            for way in range(2):
                sent(res, ag_send.at[way])

    for i in range(3):
        for copy in along_x(i):
            copy.wait_send()
    for half in range(2):
        for copy in along_y(half):
            copy.wait_send()
    last.wait()
    dx_ref[...] = (sz[0] + rz[...])[:ROWS].astype(BF16)


def local(inputs, w_gate, w_up, w_down, out_grad, confidence):
    depth, width = w_gate.shape
    vmem = pl.BlockSpec(memory_space=pltpu.VMEM)
    hbm = pl.BlockSpec(memory_space=pltpu.HBM)
    slots = (2, NY, NX, 2, SLOT, depth)
    wide = (3, TOKENS, width)
    dma = pltpu.SemaphoreType.DMA
    grad_x, grad_gate, grad_up, grad_down = pl.pallas_call(
        kernel,
        out_shape=(
            jax.ShapeDtypeStruct(inputs.shape, BF16),
            jax.ShapeDtypeStruct(w_gate.shape, BF16),
            jax.ShapeDtypeStruct(w_up.shape, BF16),
            jax.ShapeDtypeStruct((depth, width), BF16),
        ),
        in_specs=[vmem] * 3 + [hbm] * 3,
        out_specs=(vmem,) * 4,
        scratch_shapes=[
            pltpu.VMEM((HALF, HALF // ROWS * SLOT), BF16),
            pltpu.VMEM((HALF // ROWS * SLOT, HALF), BF16),
            pltpu.VMEM((SLOT, depth), BF16),
            pltpu.VMEM((SLOT, depth), BF16),
            pltpu.VMEM(slots, BF16),
            pltpu.VMEM(slots, BF16),
            pltpu.VMEM((2, TOKENS, depth), BF16),
            pltpu.VMEM((2, TOKENS, depth), BF16),
            pltpu.VMEM((2, 3, depth, width), BF16),
            pltpu.VMEM(wide, F32),
            pltpu.VMEM(wide, BF16),
            pltpu.VMEM(wide, BF16),
            pltpu.VMEM(wide, BF16),
            pltpu.VMEM(wide, BF16),
            pltpu.VMEM((2, NY, NX, SLOT, depth), BF16),
            pltpu.VMEM((2, NX - 1, NY, SLOT, depth), BF16),
            pltpu.VMEM((2, NY, SLOT, depth), F32),
            pltpu.VMEM((2, NY - 1, SLOT, depth), F32),
            pltpu.VMEM((2, SLOT, depth), F32),
            pltpu.VMEM((SLOT, depth), F32),
            dma((3,)),
            dma((2,)),
            dma((2, 2)),
            dma((2, 2, 2)),
            dma((2, 2, 2, NX - 1)),
            dma((2, 2, NX)),
            dma((2, 2, NX)),
            dma((2, 2)),
            dma,
            dma((BLOCKS, MATRICES)),
            dma((BLOCKS, MATRICES)),
            dma((2,)),
            dma((BLOCKS, MATRICES)),
            dma((3, 2, NX - 1)),
            dma((2, 2, NY - 1)),
            dma((2,)),
        ],
        compiler_params=pltpu.CompilerParams(
            collective_id=0, has_side_effects=True, vmem_limit_bytes=52 << 20
        ),
        cost_estimate=pl.CostEstimate(
            flops=2 * TOKENS * depth * width * 11,
            bytes_accessed=12 * depth * width,
            transcendentals=0,
        ),
    )(
        inputs,
        out_grad,
        confidence[None, :],
        w_gate,
        w_up,
        w_down.T,
    )
    return grad_x, grad_gate, grad_up, grad_down.T


def solution(mesh):
    placed = (
        P("dp", "tensor"),
        P("tensor", "dp"),
        P("tensor", "dp"),
        P("dp", "tensor"),
        P("dp", "tensor"),
        P("dp"),
    )
    return jax.shard_map(
        local,
        mesh=mesh,
        in_specs=placed,
        out_specs=(P("dp", "tensor"), P("tensor", "dp"), P("tensor", "dp"), P("dp", "tensor")),
        check_vma=False,
    )
```
